256 devices in a mesh: ctx: 32 (over z, y_hi, core), kvh: 8 (over x, y_lo).
Axes of the slice: x: 4, y: 4 (y_hi: 2, y_lo: 2; y = y_hi * 2 + y_lo), z: 8, core: 2. Of those that a mesh axis runs over, the one named last changes fastest.
Arguments:
- queries: bfloat16 [512, 8192], P('ctx', 'kvh'), may hold values from -200 to 200
- cache_keys: bfloat16 [65536, 1024], P('ctx', 'kvh'), may hold values from -7 to 7
- prefix_values: bfloat16 [65536, 1024], P('ctx', 'kvh'), may hold values from -6 to 6
- candidate_row_keys: bfloat16 [512, 1024], P('ctx', 'kvh'), may hold values from -12 to 12
- candidate_values: bfloat16 [512, 1024], P('ctx', 'kvh'), may hold values from -6 to 6
- prefix_len: int32 [512], P('ctx'), may hold values from 16384 to 65536, as said below
- branch: int32 [512], P('ctx'), may hold values from 0 to 127
- depth: int32 [512], P('ctx'), may hold values from 0 to 15
- out_weight: bfloat16 [8192, 8192], P('kvh', 'ctx'), may hold values from -0.625 to 0.625
Outputs:
- projected: bfloat16 [512, 8192], P('kvh', 'ctx')
The draws below stay inside these ranges and needn't reach their ends.
Inputs may be any that keep to these rules, and one draw needn't show every extreme that they name: `prefix_len`: the 16 rows of each index of ctx share a longest length, which differs from index to index; some row has length 65536.
All inputs are finite; a program needn't handle non-finite values.
Results may differ from the reference program's by a relative error of at most 0.015.
Values may be sent and summed in bfloat16 or wider, within the bound.
A program may use at most 64 MiB of HBM per device.

```python
import math
import jax
import jax.numpy as jnp
from jax import lax

D = 8192
QUERY_HEADS = 64
KEY_VALUE_HEADS = 8
HEAD_SIZE = 128
QUERY_PER_KV = 8
ROWS_DEV = 16
CACHE_POSITIONS = 65536
CANDIDATE_ROWS = 512
BRANCHES = 128


def cache_base(key):
    return jnp.clip(jax.random.normal(key, (CACHE_POSITIONS, KEY_VALUE_HEADS * HEAD_SIZE), jnp.float32), -6.0, 6.0)


def branch_ids(key):
    ids = jax.random.randint(jax.random.fold_in(key, 7), (CANDIDATE_ROWS,), 0, BRANCHES, dtype=jnp.int32)
    ids = ids.at[0].set(BRANCHES - 1)
    ids = ids.at[1].set(0)
    return ids.astype(jnp.int32)


def branch_rows(key):
    directions = jnp.clip(jax.random.normal(jax.random.fold_in(key, 8), (BRANCHES, KEY_VALUE_HEADS * HEAD_SIZE), jnp.float32), -3.0, 3.0)
    return directions[branch_ids(key)]


def block_tops(key):
    key = jax.random.fold_in(key, 13)
    count = CANDIDATE_ROWS // ROWS_DEV
    lowest = CACHE_POSITIONS // 4
    ranks = jax.random.permutation(jax.random.fold_in(key, 1), count).astype(jnp.int32)
    return (lowest + (CACHE_POSITIONS - lowest) * ranks // (count - 1)).astype(jnp.int32)


def draw_branch(key, part):
    return branch_ids(key)


def draw_queries(key, part):
    shared = branch_rows(key)
    shared = jnp.broadcast_to(shared.reshape(CANDIDATE_ROWS, KEY_VALUE_HEADS, 1, HEAD_SIZE), (CANDIDATE_ROWS, KEY_VALUE_HEADS, QUERY_PER_KV, HEAD_SIZE)).reshape(CANDIDATE_ROWS, QUERY_HEADS * HEAD_SIZE)
    key = jax.random.fold_in(key, 11)
    values = shared + jnp.clip(jax.random.normal(key, (CANDIDATE_ROWS, QUERY_HEADS * HEAD_SIZE), jnp.float32), -6.0, 6.0) * 2.0
    return values.astype(jnp.bfloat16)


def draw_candidate_row_keys(key, part):
    shared = branch_rows(key)
    key = jax.random.fold_in(key, 14)
    coefficient = (math.log(CACHE_POSITIONS) + 2.0) / math.sqrt(HEAD_SIZE)
    noise = jnp.clip(jax.random.normal(key, (CANDIDATE_ROWS, KEY_VALUE_HEADS * HEAD_SIZE), jnp.float32), -4.0, 4.0)
    values = coefficient * shared + 0.6 * noise
    return values.astype(jnp.bfloat16)


def draw_cache_keys(key, part):
    base = cache_base(key)
    tops = block_tops(key)
    shared = branch_rows(key)
    values = base
    count = CANDIDATE_ROWS // ROWS_DEV
    offsets = jnp.arange(4, dtype=jnp.int32)
    spots = (tops[:, None] - 1 - offsets[None, :]).reshape(count * 4).astype(jnp.int32)
    leaders = shared[jnp.arange(count, dtype=jnp.int32) * ROWS_DEV]
    strength = 1.6 + 0.2 * offsets.astype(jnp.float32)
    planted = strength[None, :, None] * leaders[:, None, :] + 0.3 * base[spots].reshape(count, 4, KEY_VALUE_HEADS * HEAD_SIZE)
    planted = jnp.clip(planted.reshape(count * 4, KEY_VALUE_HEADS * HEAD_SIZE), -7.0, 7.0)
    values = values.at[spots].set(planted)
    return values.astype(jnp.bfloat16)


def draw_prefix_len(key, part):
    per_block = block_tops(key)
    key = jax.random.fold_in(key, 13)
    lowest = CACHE_POSITIONS // 4
    per_row = jnp.repeat(per_block, ROWS_DEV)
    spans = per_row - lowest + 1
    raw = jax.random.randint(jax.random.fold_in(key, 2), (CANDIDATE_ROWS,), 0, 1 << 30, dtype=jnp.int32)
    lengths = lowest + raw % spans
    row_ids = jnp.arange(CANDIDATE_ROWS, dtype=jnp.int32)
    lengths = jnp.where(row_ids % ROWS_DEV == 0, per_row, lengths)
    return lengths.astype(jnp.int32)


def plant(drawn, key, smallest, largest):
    dims = drawn.shape
    place = [jax.random.randint(jax.random.fold_in(key, axis), (), 0, dims[axis]) for axis in range(len(dims))]
    drawn = drawn.at[tuple(place)].set(smallest)
    longest = dims.index(max(dims))
    place[longest] = (place[longest] + 1) % dims[longest]
    return drawn.at[tuple(place)].set(largest)


def levels(own_key, extent, shards, smallest, high):
    factor_of = 1.0
    for position, blocks in shards:
        heights = jax.random.uniform(jax.random.fold_in(jax.random.fold_in(own_key, 6), position), (blocks,), jnp.float32, smallest / len(shards), high / len(shards))
        factor_of = factor_of * jnp.repeat(jnp.exp(heights), extent[position] // blocks).reshape((-1,) + (1,) * (len(extent) - 1 - position))
    return factor_of


def gaussian(key, dims, spread, limit, pieces=(), kind=jnp.bfloat16):
    result = spread * jax.random.normal(key, dims, jnp.float32)
    if pieces:
        result = result * levels(key, dims, pieces, -0.22, 0.18)
    return jnp.clip(result, -limit, limit).astype(kind)


def setup_inputs(seed: int = 0) -> dict:
    seeds = jax.random.split(jax.random.key(seed), 10)
    return {
        "queries": draw_queries(jax.random.fold_in(seeds[9], 71), 0),
        "cache_keys": draw_cache_keys(jax.random.fold_in(seeds[9], 71), 0),
        "prefix_values": gaussian(seeds[2], (CACHE_POSITIONS, KEY_VALUE_HEADS * HEAD_SIZE), 1.0, 6.0, ((0, 32), (1, 8))),
        "candidate_row_keys": draw_candidate_row_keys(jax.random.fold_in(seeds[9], 71), 0),
        "candidate_values": gaussian(seeds[4], (CANDIDATE_ROWS, KEY_VALUE_HEADS * HEAD_SIZE), 1.0, 6.0, ((0, 32), (1, 8))),
        "prefix_len": draw_prefix_len(jax.random.fold_in(seeds[9], 71), 0),
        "branch": draw_branch(jax.random.fold_in(seeds[9], 71), 0),
        "depth": plant(jax.random.randint(seeds[7], (CANDIDATE_ROWS,), 0, 16), jax.random.fold_in(seeds[7], 1), 0, 15).astype(jnp.int32),
        "out_weight": gaussian(seeds[8], (QUERY_HEADS * HEAD_SIZE, D), 0.04, 0.625, ((0, 8), (1, 32))),
    }


def reference(queries, cache_keys, prefix_values, candidate_row_keys, candidate_values, prefix_len, branch, depth, out_weight):
    scale = 1.0 / math.sqrt(HEAD_SIZE)
    block = 32
    positions = jnp.arange(CACHE_POSITIONS, dtype=jnp.int32)

    def group_function(g):
        g = g.astype(jnp.int32)
        keys_c = lax.dynamic_slice_in_dim(cache_keys, g * HEAD_SIZE, HEAD_SIZE, 1).astype(jnp.float32)
        vals_c = lax.dynamic_slice_in_dim(prefix_values, g * HEAD_SIZE, HEAD_SIZE, 1).astype(jnp.float32)
        keys_n = lax.dynamic_slice_in_dim(candidate_row_keys, g * HEAD_SIZE, HEAD_SIZE, 1).astype(jnp.float32)
        vals_n = lax.dynamic_slice_in_dim(candidate_values, g * HEAD_SIZE, HEAD_SIZE, 1).astype(jnp.float32)
        q_group = lax.dynamic_slice_in_dim(queries, g * QUERY_PER_KV * HEAD_SIZE, QUERY_PER_KV * HEAD_SIZE, 1).reshape(CANDIDATE_ROWS, QUERY_PER_KV, HEAD_SIZE)

        def block_fn(b):
            first = (b * block).astype(jnp.int32)
            q_rows = lax.dynamic_slice_in_dim(q_group, first, block, 0).astype(jnp.float32)
            lengths = lax.dynamic_slice_in_dim(prefix_len, first, block, 0)
            own_branch = lax.dynamic_slice_in_dim(branch, first, block, 0)
            own_depth = lax.dynamic_slice_in_dim(depth, first, block, 0)
            s_cache = jnp.einsum('rgd,sd->rgs', q_rows, keys_c) * scale
            mask_cache = (positions[None, :] < lengths[:, None])[:, None, :]
            s_cand = jnp.einsum('rgd,nd->rgn', q_rows, keys_n) * scale
            mask_cand = ((branch[None, :] == own_branch[:, None]) & (depth[None, :] <= own_depth[:, None]))[:, None, :]
            s_cache = jnp.where(mask_cache, s_cache, -jnp.inf)
            s_cand = jnp.where(mask_cand, s_cand, -jnp.inf)
            top = jnp.maximum(lax.optimization_barrier(jnp.max(s_cache, axis=-1)), lax.optimization_barrier(jnp.max(s_cand, axis=-1)))
            p_cache = jnp.exp(s_cache - top[..., None])
            p_cand = jnp.exp(s_cand - top[..., None])
            total = lax.optimization_barrier(jnp.sum(p_cache, axis=-1)) + lax.optimization_barrier(jnp.sum(p_cand, axis=-1))
            w_cache = lax.optimization_barrier(p_cache.astype(jnp.bfloat16)).astype(jnp.float32)
            w_cand = lax.optimization_barrier(p_cand.astype(jnp.bfloat16)).astype(jnp.float32)
            numer = jnp.einsum('rgs,sd->rgd', w_cache, vals_c) + jnp.einsum('rgn,nd->rgd', w_cand, vals_n)
            return (numer / total[..., None]).astype(jnp.bfloat16)
        blocks = lax.map(block_fn, jnp.arange(CANDIDATE_ROWS // block, dtype=jnp.int32))
        return blocks.reshape(CANDIDATE_ROWS, QUERY_PER_KV * HEAD_SIZE)
    head_groups = lax.map(group_function, jnp.arange(KEY_VALUE_HEADS, dtype=jnp.int32))
    attn = jnp.transpose(head_groups, (1, 0, 2)).reshape(CANDIDATE_ROWS, QUERY_HEADS * HEAD_SIZE)
    return jnp.dot(attn, out_weight, preferred_element_type=jnp.float32).astype(jnp.bfloat16)
```

```python
import math

import jax
import jax.numpy as jnp
from jax import lax
from jax.experimental import pallas as pl
from jax.experimental.pallas import tpu as pltpu
from jax.sharding import PartitionSpec as P

MESH = pl.DeviceIdType.MESH
BF = jnp.bfloat16
F32 = jnp.float32
HEAD = 128
HEADS = 8
ROWS = 16
RINGZ = 8
SHARD = 2048
PAIR = 2 * SHARD
CAND = 2 * ROWS
KPOS = PAIR + CAND
VPOS = PAIR + 128
QH = HEADS * ROWS
QW = HEADS * HEAD + 128
BLK = HEAD + 16
COLS = 256
NEG = -1e30
SCALE = math.log2(math.e) / math.sqrt(HEAD)
CQ = 256
CP = 1024


def split2(x):
    hi = x.astype(BF)
    lo = (x - hi.astype(F32)).astype(BF)
    return hi, lo


def kernel(
    q_hbm, k_hbm, v_hbm, ck_hbm, cv_hbm, len_s, branch_s, depth_s, w_hbm,
    out_ref,
    qall, kbuf, vraw, vt, cvraw, cinfo, wbuf, sa, sb, pbuf, ma, mb, part, got, blk, attn, prod, terms,
    loc, kv_s, kv_r, q_s, q_r, p_s, p_r, a_s, a_r, t_s, t_r,
):
    ctx = lax.axis_index("ctx")
    kvh = lax.axis_index("kvh")
    z = ctx // 4
    yh = (ctx // 2) % 2
    core = ctx % 2

    def plane(dz, so):
        zz = (z + dz) % RINGZ
        yy = (yh + so) % 2
        return (zz * 4 + yy * 2 + core, kvh)

    sibling = (ctx + 1 - 2 * core, kvh)

    def head_group(k, c):
        return (ctx - core + c, k)

    bar = pltpu.get_barrier_semaphore()
    for dz in range(RINGZ):
        for so in range(2):
            if dz or so:
                pl.semaphore_signal(bar, inc=1, device_id=plane(dz, so), device_id_type=MESH)
    pl.semaphore_signal(bar, inc=1, device_id=sibling, device_id_type=MESH)
    for dk in range(1, RINGZ):
        for c in range(2):
            pl.semaphore_signal(
                bar, inc=1, device_id=head_group((kvh + dk) % RINGZ, c), device_id_type=MESH
            )

    mine = pl.multiple_of(core * SHARD, SHARD)
    cmine = pl.multiple_of(PAIR + core * ROWS, ROWS)
    crow = pl.multiple_of(core * ROWS, ROWS)
    wmine = pl.multiple_of(core * COLS, COLS)
    loads = [
        pltpu.make_async_copy(q_hbm, qall.at[0, 0, :, pl.ds(0, HEADS * HEAD)], loc.at[0]),
        pltpu.make_async_copy(k_hbm, kbuf.at[pl.ds(mine, SHARD)], loc.at[1]),
        pltpu.make_async_copy(v_hbm, vraw, loc.at[2]),
        pltpu.make_async_copy(ck_hbm, kbuf.at[pl.ds(cmine, ROWS)], loc.at[3]),
        pltpu.make_async_copy(cv_hbm, cvraw.at[pl.ds(crow, ROWS)], loc.at[4]),
        pltpu.make_async_copy(w_hbm, wbuf.at[:, pl.ds(wmine, COLS)], loc.at[5]),
    ]
    for copy in loads:
        copy.start()

    lane = lax.broadcasted_iota(jnp.int32, (ROWS, QH), 1)
    sub = lax.broadcasted_iota(jnp.int32, (ROWS, QH), 0)
    lane_row = lane % ROWS
    meta = jnp.zeros((ROWS, QH), jnp.int32)
    cb = jnp.zeros((ROWS, QH), jnp.int32)
    cd = jnp.zeros((ROWS, QH), jnp.int32)
    for i in range(ROWS):
        n = len_s[i]
        b = branch_s[i]
        d = depth_s[i]
        high = n // 256
        col = jnp.where(
            sub == 0, high, jnp.where(sub == 1, n - high * 256, jnp.where(sub == 2, b, d))
        )
        meta = jnp.where(lane_row == i, col, meta)
        cb = jnp.where(sub == i, b, cb)
        cd = jnp.where(sub == i, d, cd)
    qall[0, 0, :, HEADS * HEAD :] = meta.astype(F32).astype(BF)
    cinfo[core, 0] = cb.astype(F32).astype(BF)
    cinfo[core, 1] = cd.astype(F32).astype(BF)
    pbuf[KPOS:, :] = jnp.zeros((VPOS - KPOS, 2 * QH), BF)
    vt[HEAD:, :] = jnp.ones((BLK - HEAD, VPOS), BF)
    cvraw[CAND:, :] = jnp.zeros((128 - CAND, HEAD), BF)
    for copy in loads:
        copy.wait()
    for j in range(0, SHARD, 128):
        vt[0:HEAD, pl.ds(pl.multiple_of(mine + j, 128), 128)] = vraw[j : j + 128, :].T

    pl.semaphore_wait(bar, 30)

    def swap(n, ref):
        return pltpu.make_async_remote_copy(
            src_ref=ref, dst_ref=ref, send_sem=kv_s.at[n], recv_sem=kv_r.at[n],
            device_id=sibling, device_id_type=MESH,
        )

    def swaps(side):
        base = pl.multiple_of(side * SHARD, SHARD)
        cbase = pl.multiple_of(PAIR + side * ROWS, ROWS)
        rbase = pl.multiple_of(side * ROWS, ROWS)
        wbase = pl.multiple_of(side * COLS, COLS)
        return [
            swap(0, kbuf.at[pl.ds(base, SHARD)]),
            swap(1, kbuf.at[pl.ds(cbase, ROWS)]),
            swap(2, cvraw.at[pl.ds(rbase, ROWS)]),
            swap(3, cinfo.at[side]),
            swap(4, vt.at[pl.ds(0, HEAD), pl.ds(base, SHARD)]),
            swap(5, wbuf.at[:, pl.ds(wbase, COLS)]),
        ]

    def around(dz, so, src, dst, send, recv):
        back = (RINGZ - dz) % RINGZ
        return pltpu.make_async_remote_copy(
            src_ref=src, dst_ref=dst.at[back, so], send_sem=send.at[dz * 2 + so],
            recv_sem=recv.at[back * 2 + so], device_id=plane(dz, so), device_id_type=MESH,
        )

    def arrival(dz, so, dst, recv):
        return pltpu.make_async_remote_copy(
            src_ref=dst.at[dz, so], dst_ref=dst.at[dz, so], send_sem=recv.at[dz * 2 + so],
            recv_sem=recv.at[dz * 2 + so], device_id=plane(dz, so), device_id_type=MESH,
        )

    order = [1, 7, 2, 6, 3, 5, 4, 0]
    q_out = []
    for dz in order:
        for so in range(2):
            if dz or so:
                copy = around(dz, so, qall.at[0, 0], qall, q_s, q_r)
                copy.start()
                q_out.append(copy)
    out_swaps = swaps(core)
    in_swaps = swaps(1 - core)
    for copy in out_swaps:
        copy.start()
    for n in range(4):
        in_swaps[n].wait_recv()

    base = (ctx - core) * SHARD
    pos_sub = lax.broadcasted_iota(jnp.int32, (CQ, QH), 0)

    def offset(t):
        return (((t // 2) + 1) * (1 - 2 * (t % 2)) + RINGZ) % RINGZ

    def load_q(dz):
        parts = []
        infos = []
        for so in range(2):
            for h in range(HEADS):
                parts.append(qall[dz, so, :, h * HEAD : (h + 1) * HEAD])
            infos.append(qall[dz, so, :, HEADS * HEAD :].astype(F32))
        q = jnp.concatenate(parts, axis=0).astype(F32) * SCALE
        hi, lo = split2(q)
        lens = [(f[0:1] * 256.0 + f[1:2]).astype(jnp.int32) - base for f in infos]
        return jnp.concatenate([hi, lo], axis=1), lens, infos

    def score(q, pos, width):
        k = kbuf[pos : pos + width, :]
        return lax.dot_general(
            jnp.concatenate([k, k], axis=1), q, (((1,), (1,)), ((), ())),
            preferred_element_type=F32,
        )

    def fused(dz_new, dz_old, parity):
        s_new, s_old = (sa, sb) if parity == 0 else (sb, sa)
        m_new, m_old = (ma, mb) if parity == 0 else (mb, ma)
        if dz_new is not None:
            q, lens, infos = load_q(dz_new)
            top = jnp.full((8, 2 * QH), NEG, F32)
            s = score(q, PAIR, CAND)
            cbr = jnp.concatenate([cinfo[0, 0], cinfo[1, 0]], axis=0).astype(F32)
            cde = jnp.concatenate([cinfo[0, 1], cinfo[1, 1]], axis=0).astype(F32)
            s = jnp.concatenate(
                [
                    jnp.where(
                        (cbr == f[2:3]) & (cde <= f[3:4]), s[:, n * QH : (n + 1) * QH], NEG
                    )
                    for n, f in enumerate(infos)
                ],
                axis=1,
            )
            s_new[PAIR:KPOS, :] = s
            for j in range(0, CAND, 8):
                top = jnp.maximum(top, s[j : j + 8, :])
        if dz_old is not None:
            m = m_old[0:1, :]
            acc = None
            start = 0
        for pos in range(0, PAIR, CQ):
            if dz_new is not None:
                s = score(q, pos, CQ)
                s = jnp.concatenate(
                    [
                        jnp.where(pos_sub < n - pos, s[:, j * QH : (j + 1) * QH], NEG)
                        for j, n in enumerate(lens)
                    ],
                    axis=1,
                )
                s_new[pos : pos + CQ, :] = s
                for j in range(0, CQ, 8):
                    top = jnp.maximum(top, s[j : j + 8, :])
            if dz_old is not None:
                pbuf[pos : pos + CQ, :] = jnp.exp2(s_old[pos : pos + CQ, :] - m).astype(BF)
                end = pos + CQ
                if end == PAIR:
                    pbuf[PAIR:KPOS, :] = jnp.exp2(s_old[PAIR:KPOS, :] - m).astype(BF)
                    end = VPOS
                if end - start >= CP:
                    term = jnp.dot(
                        vt[:, start:end], pbuf[start:end, :], preferred_element_type=F32
                    )
                    acc = term if acc is None else acc + term
                    start = end
        if dz_old is not None:
            total = acc[HEAD : HEAD + 1]
            m_hi, rest = m.astype(BF), m - m.astype(BF).astype(F32)
            m_mid, m_lo = split2(rest)
            l_hi, l_lo = split2(total)
            row = lax.broadcasted_iota(jnp.int32, (BLK - HEAD, 2 * QH), 0)
            stats = jnp.zeros((BLK - HEAD, 2 * QH), F32)
            for n, x in enumerate((m_hi, m_mid, m_lo, l_hi, l_lo)):
                stats = jnp.where(row == n, x.astype(F32), stats)
            for so in range(2):
                lanes = slice(so * QH, (so + 1) * QH)
                part[dz_old, so, 0:HEAD, :] = acc[0:HEAD, lanes].astype(BF)
                part[dz_old, so, HEAD:, :] = stats[:, lanes].astype(BF)
        if dz_new is not None:
            m_new[...] = jnp.broadcast_to(jnp.max(top, axis=0, keepdims=True), (8, 2 * QH))

    def send_part(dz):
        back = (RINGZ - dz) % RINGZ
        for so in range(2):
            pltpu.make_async_remote_copy(
                src_ref=part.at[dz, so], dst_ref=got.at[back, so], send_sem=p_s.at[dz * 2 + so],
                recv_sem=p_r.at[back * 2 + so], device_id=plane(dz, so), device_id_type=MESH,
            ).start()

    def arrive_q(dz):
        for so in range(2):
            arrival(dz, so, qall, q_r).wait_recv()

    arrive_q(1)
    fused(1, None, 0)
    in_swaps[4].wait_recv()
    vt[0:HEAD, PAIR:] = cvraw[...].T

    def body(i, carry):
        a, b, c = offset(2 * i), offset(2 * i + 1), offset(2 * i + 2)
        arrive_q(b)
        fused(b, a, 1)
        send_part(a)
        arrive_q(c)
        fused(c, b, 0)
        send_part(b)
        return carry

    lax.fori_loop(0, 3, body, 0)
    arrival(0, 1, qall, q_r).wait_recv()
    fused(0, 4, 1)
    send_part(4)
    fused(None, 0, 0)
    other = around(0, 1, part.at[0, 1], got, p_s, p_r)
    other.start()
    got[0, 0] = part[0, 0]

    for dz in range(RINGZ):
        for so in range(2):
            if dz or so:
                arrival(dz, so, got, p_r).wait_recv()
    tops = []
    totals = []
    for dz in range(RINGZ):
        for so in range(2):
            st = got[dz, so, HEAD:, :].astype(F32)
            tops.append(st[0:1] + st[1:2] + st[2:3])
            totals.append(st[3:4] + st[4:5])
    top = tops[0]
    for x in tops[1:]:
        top = jnp.maximum(top, x)
    acc = jnp.zeros((HEAD, QH), F32)
    total = jnp.zeros((1, QH), F32)
    for n in range(2 * RINGZ):
        f = jnp.exp2(tops[n] - top)
        total = total + totals[n] * f
        acc = acc + got[n // 2, n % 2, 0:HEAD, :].astype(F32) * f
    own = (acc / total).T.astype(BF)
    for h in range(HEADS):
        blk[:, h * HEAD : (h + 1) * HEAD] = own[h * ROWS : (h + 1) * ROWS, :]
    a_out = []
    for dz in (4, 3, 5, 2, 6, 1, 7, 0):
        for so in range(2):
            if dz or so:
                copy = around(dz, so, blk, attn, a_s, a_r)
                copy.start()
                a_out.append(copy)
    attn[0, 0] = blk[...]

    in_swaps[5].wait_recv()
    me = kvh * 2 + core

    def term_copy(n, k, c):
        return pltpu.make_async_remote_copy(
            src_ref=prod.at[n, c], dst_ref=terms.at[me], send_sem=t_s.at[n * 2 + c],
            recv_sem=t_r.at[me], device_id=head_group(k, c), device_id_type=MESH,
        )

    for n in (0, 1, 7, 2, 6, 3, 5, 4):
        for so in range(2):
            if n or so:
                arrival(n, so, attn, a_r).wait_recv()
        rows = jnp.concatenate([attn[n, 0], attn[n, 1]], axis=0)
        res = jnp.dot(rows, wbuf[...], preferred_element_type=F32).astype(BF)
        k = (z + n) % RINGZ
        for c in range(2):
            prod[n, c] = res[:, c * COLS : (c + 1) * COLS]
        for c in range(2):
            here = (k == kvh) & (core == c)

            @pl.when(here)
            def _():
                terms[me] = prod[n, c]

            @pl.when(jnp.logical_not(here))
            def _():
                term_copy(n, k, c).start()

    for k in range(RINGZ):
        for c in range(2):
            idx = k * 2 + c

            @pl.when(idx != me)
            def _():
                pltpu.make_async_remote_copy(
                    src_ref=terms.at[idx], dst_ref=terms.at[idx], send_sem=t_r.at[idx],
                    recv_sem=t_r.at[idx], device_id=sibling, device_id_type=MESH,
                ).wait_recv()

    for c in range(2):
        res = terms[c].astype(F32)
        for k in range(1, RINGZ):
            res = res + terms[k * 2 + c].astype(F32)
        res = res.astype(BF)
        for so in range(2):
            row = pl.multiple_of(((yh + so) % 2) * CAND + c * ROWS, ROWS)
            out_ref[pl.ds(row, ROWS), :] = res[so * ROWS : (so + 1) * ROWS, :]

    for copy in q_out + out_swaps + a_out:
        copy.wait_send()
    for dz in range(RINGZ):
        for so in range(2):
            if dz or so:
                around(dz, so, part.at[dz, so], got, p_s, p_r).wait_send()
    for n in range(RINGZ):
        k = (z + n) % RINGZ
        for c in range(2):

            @pl.when(jnp.logical_not((k == kvh) & (core == c)))
            def _():
                term_copy(n, k, c).wait_send()


def local(q, k, v, ck, cv, length, branch, depth, w):
    hbm = pl.BlockSpec(memory_space=pl.ANY)
    smem = pl.BlockSpec(memory_space=pltpu.SMEM)
    dma = pltpu.SemaphoreType.DMA
    return pl.pallas_call(
        kernel,
        out_shape=jax.ShapeDtypeStruct((4 * ROWS, COLS), BF),
        in_specs=[hbm] * 5 + [smem] * 3 + [hbm],
        out_specs=pl.BlockSpec(memory_space=pltpu.VMEM),
        scratch_shapes=[
            pltpu.VMEM((RINGZ, 2, ROWS, QW), BF),
            pltpu.VMEM((KPOS, HEAD), BF),
            pltpu.VMEM((SHARD, HEAD), BF),
            pltpu.VMEM((BLK, VPOS), BF),
            pltpu.VMEM((128, HEAD), BF),
            pltpu.VMEM((2, 2, ROWS, QH), BF),
            pltpu.VMEM((HEADS * HEAD, 2 * COLS), BF),
            pltpu.VMEM((KPOS, 2 * QH), F32),
            pltpu.VMEM((KPOS, 2 * QH), F32),
            pltpu.VMEM((VPOS, 2 * QH), BF),
            pltpu.VMEM((8, 2 * QH), F32),
            pltpu.VMEM((8, 2 * QH), F32),
            pltpu.VMEM((RINGZ, 2, BLK, QH), BF),
            pltpu.VMEM((RINGZ, 2, BLK, QH), BF),
            pltpu.VMEM((ROWS, HEADS * HEAD), BF),
            pltpu.VMEM((RINGZ, 2, ROWS, HEADS * HEAD), BF),
            pltpu.VMEM((RINGZ, 2, 2 * ROWS, COLS), BF),
            pltpu.VMEM((2 * RINGZ, 2 * ROWS, COLS), BF),
            dma((6,)), dma((6,)), dma((6,)),
            dma((16,)), dma((16,)), dma((16,)), dma((16,)),
            dma((16,)), dma((16,)), dma((16,)), dma((16,)),
        ],
        compiler_params=pltpu.CompilerParams(
            collective_id=0, has_side_effects=True, vmem_limit_bytes=48 * 2**20
        ),
        cost_estimate=pl.CostEstimate(
            flops=9 * 10**9, bytes_accessed=2 * 2**20, transcendentals=2048 * 4224
        ),
    )(q, k, v, ck, cv, length, branch, depth, w)


def solution(mesh):
    in_specs = (
        P("ctx", "kvh"),
        P("ctx", "kvh"),
        P("ctx", "kvh"),
        P("ctx", "kvh"),
        P("ctx", "kvh"),
        P("ctx"),
        P("ctx"),
        P("ctx"),
        P("kvh", "ctx"),
    )
    return jax.shard_map(
        local, mesh=mesh, in_specs=in_specs, out_specs=P("kvh", "ctx"), check_vma=False
    )
```

```python
import math

import jax
import jax.numpy as jnp
from jax import lax
from jax.experimental import pallas as pl
from jax.experimental.pallas import tpu as pltpu
from jax.sharding import PartitionSpec as P

MESH = pl.DeviceIdType.MESH
BF = jnp.bfloat16
F32 = jnp.float32
HEAD = 128
HEADS = 8
ROWS = 16
RINGZ = 8
SHARD = 2048
PAIR = 2 * SHARD
CAND = 2 * ROWS
KPOS = PAIR + CAND
VPOS = PAIR + 128
QH = HEADS * ROWS
QW = HEADS * HEAD + 128
BLK = HEAD + 16
COLS = 256
NEG = -1e30
SCALE = math.log2(math.e) / math.sqrt(HEAD)
CQ = 256
CP = 1024
WROWS = HEADS * HEAD // RINGZ


def split2(x):
    hi = x.astype(BF)
    lo = (x - hi.astype(F32)).astype(BF)
    return hi, lo


def kernel(
    q_hbm, k_hbm, v_hbm, ck_hbm, cv_hbm, len_s, branch_s, depth_s, w_hbm,
    out_ref,
    qall, kbuf, vraw, vt, cvraw, cinfo, wbuf, sa, sb, pbuf, ma, mb, part, got, ysend, yget, blk, attn, prod, terms,
    loc, kv_s, kv_r, w_s, w_r, q_s, q_r, p_s, p_r, y_s, y_r, a_s, a_r, t_s, t_r,
):
    ctx = lax.axis_index("ctx")
    kvh = lax.axis_index("kvh")
    z = ctx // 4
    yh = (ctx // 2) % 2
    core = ctx % 2
    quarter = ctx % 4
    partner = (quarter + 2) % 4

    def plane(dz, so):
        zz = (z + dz) % RINGZ
        yy = (yh + so) % 2
        return (zz * 4 + yy * 2 + core, kvh)

    sibling = (ctx + 1 - 2 * core, kvh)

    def group(j, k):
        return (ctx - quarter + j, k)

    bar = pltpu.get_barrier_semaphore()
    peers = [plane(dz, 0) for dz in range(1, RINGZ)] + [plane(1, 1), plane(RINGZ - 1, 1)]
    peers += [group((quarter + j) % 4, kvh) for j in range(1, 4)]
    peers += [group(j, (kvh + dk) % RINGZ) for dk in range(1, RINGZ) for j in range(4)]
    for peer in peers:
        pl.semaphore_signal(bar, inc=1, device_id=peer, device_id_type=MESH)

    mine = pl.multiple_of(core * SHARD, SHARD)
    cmine = pl.multiple_of(PAIR + core * ROWS, ROWS)
    crow = pl.multiple_of(core * ROWS, ROWS)
    loads = [
        pltpu.make_async_copy(q_hbm, qall.at[0, 0, :, pl.ds(0, HEADS * HEAD)], loc.at[0]),
        pltpu.make_async_copy(k_hbm, kbuf.at[pl.ds(mine, SHARD)], loc.at[1]),
        pltpu.make_async_copy(v_hbm, vraw, loc.at[2]),
        pltpu.make_async_copy(ck_hbm, kbuf.at[pl.ds(cmine, ROWS)], loc.at[3]),
        pltpu.make_async_copy(cv_hbm, cvraw.at[pl.ds(crow, ROWS)], loc.at[4]),
        pltpu.make_async_copy(w_hbm, wbuf.at[quarter], loc.at[5]),
    ]
    for copy in loads:
        copy.start()

    lane = lax.broadcasted_iota(jnp.int32, (ROWS, QH), 1)
    sub = lax.broadcasted_iota(jnp.int32, (ROWS, QH), 0)
    lane_row = lane % ROWS
    meta = jnp.zeros((ROWS, QH), jnp.int32)
    cb = jnp.zeros((ROWS, QH), jnp.int32)
    cd = jnp.zeros((ROWS, QH), jnp.int32)
    for i in range(ROWS):
        n = len_s[i]
        b = branch_s[i]
        d = depth_s[i]
        high = n // 256
        col = jnp.where(
            sub == 0, high, jnp.where(sub == 1, n - high * 256, jnp.where(sub == 2, b, d))
        )
        meta = jnp.where(lane_row == i, col, meta)
        cb = jnp.where(sub == i, b, cb)
        cd = jnp.where(sub == i, d, cd)
    qall[0, 0, :, HEADS * HEAD :] = meta.astype(F32).astype(BF)
    cinfo[core, 0] = cb.astype(F32).astype(BF)
    cinfo[core, 1] = cd.astype(F32).astype(BF)
    pbuf[KPOS:, :] = jnp.zeros((VPOS - KPOS, 2 * QH), BF)
    vt[HEAD:, :] = jnp.ones((BLK - HEAD, VPOS), BF)
    cvraw[CAND:, :] = jnp.zeros((128 - CAND, HEAD), BF)
    for copy in loads:
        copy.wait()
    for j in range(0, SHARD, 128):
        vt[0:HEAD, pl.ds(pl.multiple_of(mine + j, 128), 128)] = vraw[j : j + 128, :].T

    pl.semaphore_wait(bar, len(peers))

    def swap(n, ref):
        return pltpu.make_async_remote_copy(
            src_ref=ref, dst_ref=ref, send_sem=kv_s.at[n], recv_sem=kv_r.at[n],
            device_id=sibling, device_id_type=MESH,
        )

    def swaps(side):
        base = pl.multiple_of(side * SHARD, SHARD)
        cbase = pl.multiple_of(PAIR + side * ROWS, ROWS)
        rbase = pl.multiple_of(side * ROWS, ROWS)
        return [
            swap(0, kbuf.at[pl.ds(base, SHARD)]),
            swap(1, kbuf.at[pl.ds(cbase, ROWS)]),
            swap(2, cvraw.at[pl.ds(rbase, ROWS)]),
            swap(3, cinfo.at[side]),
            swap(4, vt.at[pl.ds(0, HEAD), pl.ds(base, SHARD)]),
            swap(5, wbuf.at[quarter - core + side]),
        ]

    def arrival(dz, so, dst, recv):
        return pltpu.make_async_remote_copy(
            src_ref=dst.at[dz, so], dst_ref=dst.at[dz, so], send_sem=recv.at[dz * 2 + so],
            recv_sem=recv.at[dz * 2 + so], device_id=plane(dz, so), device_id_type=MESH,
        )

    def query_out(dz, so, fwd):
        back = (RINGZ - dz) % RINGZ
        slot = (so + fwd) % 2
        return pltpu.make_async_remote_copy(
            src_ref=qall.at[0, fwd], dst_ref=qall.at[back, slot], send_sem=q_s.at[dz * 3 + so + 2 * fwd],
            recv_sem=q_r.at[back * 2 + slot], device_id=plane(dz, so), device_id_type=MESH,
        )

    direct = [(0, 1), (1, 1), (7, 1), (1, 0), (7, 0), (2, 0), (6, 0), (3, 0), (5, 0), (4, 0)]
    q_out = [query_out(dz, so, 0) for dz, so in direct]
    for copy in q_out:
        copy.start()
    out_swaps = swaps(core)
    in_swaps = swaps(1 - core)
    for copy in out_swaps:
        copy.start()

    def w_across(n, slab):
        rows = pl.ds(n * WROWS, WROWS)
        return pltpu.make_async_remote_copy(
            src_ref=wbuf.at[slab, rows], dst_ref=wbuf.at[slab, rows], send_sem=w_s.at[n],
            recv_sem=w_r.at[n], device_id=plane(0, 1), device_id_type=MESH,
        )

    def w_relay(slab):
        return pltpu.make_async_remote_copy(
            src_ref=wbuf.at[slab], dst_ref=wbuf.at[slab], send_sem=w_s.at[RINGZ],
            recv_sem=w_r.at[RINGZ], device_id=sibling, device_id_type=MESH,
        )

    arrival(0, 1, qall, q_r).wait_recv()
    for dz in (2, 6, 3, 5, 4):
        copy = query_out(dz, 0, 1)
        copy.start()
        q_out.append(copy)
    for n in range(4):
        in_swaps[n].wait_recv()

    base = (ctx - core) * SHARD
    pos_sub = lax.broadcasted_iota(jnp.int32, (CQ, QH), 0)

    def read_stats(st):
        return st[0:1] + st[1:2] + st[2:3], st[3:4] + st[4:5]

    def write_stats(m, total):
        m_hi = m.astype(BF)
        m_mid, m_lo = split2(m - m_hi.astype(F32))
        l_hi, l_lo = split2(total)
        row = lax.broadcasted_iota(jnp.int32, (BLK - HEAD, m.shape[1]), 0)
        stats = jnp.zeros((BLK - HEAD, m.shape[1]), F32)
        for n, x in enumerate((m_hi, m_mid, m_lo, l_hi, l_lo)):
            stats = jnp.where(row == n, x.astype(F32), stats)
        return stats.astype(BF)

    def load_q(dz):
        parts = []
        infos = []
        for so in range(2):
            for h in range(HEADS):
                parts.append(qall[dz, so, :, h * HEAD : (h + 1) * HEAD])
            infos.append(qall[dz, so, :, HEADS * HEAD :].astype(F32))
        q = jnp.concatenate(parts, axis=0).astype(F32) * SCALE
        hi, lo = split2(q)
        lens = [(f[0:1] * 256.0 + f[1:2]).astype(jnp.int32) - base for f in infos]
        return jnp.concatenate([hi, lo], axis=1), lens, infos

    def score(q, pos, width):
        k = kbuf[pos : pos + width, :]
        return lax.dot_general(
            jnp.concatenate([k, k], axis=1), q, (((1,), (1,)), ((), ())),
            preferred_element_type=F32,
        )

    def fused(dz_new, dz_old, parity):
        s_new, s_old = (sa, sb) if parity == 0 else (sb, sa)
        m_new, m_old = (ma, mb) if parity == 0 else (mb, ma)
        if dz_new is not None:
            q, lens, infos = load_q(dz_new)
            top = jnp.full((8, 2 * QH), NEG, F32)
            s = score(q, PAIR, CAND)
            cbr = jnp.concatenate([cinfo[0, 0], cinfo[1, 0]], axis=0).astype(F32)
            cde = jnp.concatenate([cinfo[0, 1], cinfo[1, 1]], axis=0).astype(F32)
            s = jnp.concatenate(
                [
                    jnp.where(
                        (cbr == f[2:3]) & (cde <= f[3:4]), s[:, n * QH : (n + 1) * QH], NEG
                    )
                    for n, f in enumerate(infos)
                ],
                axis=1,
            )
            s_new[PAIR:KPOS, :] = s
            for j in range(0, CAND, 8):
                top = jnp.maximum(top, s[j : j + 8, :])
        if dz_old is not None:
            m = m_old[0:1, :]
            acc = None
            start = 0
        for pos in range(0, PAIR, CQ):
            if dz_new is not None:
                s = score(q, pos, CQ)
                s = jnp.concatenate(
                    [
                        jnp.where(pos_sub < n - pos, s[:, j * QH : (j + 1) * QH], NEG)
                        for j, n in enumerate(lens)
                    ],
                    axis=1,
                )
                s_new[pos : pos + CQ, :] = s
                for j in range(0, CQ, 8):
                    top = jnp.maximum(top, s[j : j + 8, :])
            if dz_old is not None:
                pbuf[pos : pos + CQ, :] = jnp.exp2(s_old[pos : pos + CQ, :] - m).astype(BF)
                end = pos + CQ
                if end == PAIR:
                    pbuf[PAIR:KPOS, :] = jnp.exp2(s_old[PAIR:KPOS, :] - m).astype(BF)
                    end = VPOS
                if end - start >= CP:
                    term = jnp.dot(
                        vt[:, start:end], pbuf[start:end, :], preferred_element_type=F32
                    )
                    acc = term if acc is None else acc + term
                    start = end
        if dz_old is not None:
            total = acc[HEAD : HEAD + 1]
            stats = write_stats(m, total)
            for so in range(2):
                lanes = slice(so * QH, (so + 1) * QH)
                part[dz_old, so, 0:HEAD, :] = acc[0:HEAD, lanes].astype(BF)
                part[dz_old, so, HEAD:, :] = stats[:, lanes]
        if dz_new is not None:
            m_new[...] = jnp.broadcast_to(jnp.max(top, axis=0, keepdims=True), (8, 2 * QH))

    def part_out(dz):
        back = (RINGZ - dz) % RINGZ
        return pltpu.make_async_remote_copy(
            src_ref=part.at[dz], dst_ref=got.at[back], send_sem=p_s.at[dz],
            recv_sem=p_r.at[back], device_id=plane(dz, 0), device_id_type=MESH,
        )

    def arrive_q(dz):
        for so in range(2):
            arrival(dz, so, qall, q_r).wait_recv()

    order = [1, 7, 2, 3, 5, 4, 6, 0]

    def nth(t):
        dz = jnp.int32(order[0])
        for n in range(1, RINGZ):
            dz = jnp.where(t == n, order[n], dz)
        return dz

    arrive_q(order[0])
    fused(order[0], None, 0)
    in_swaps[4].wait_recv()
    vt[0:HEAD, PAIR:] = cvraw[...].T
    w_across(0, quarter).start()
    w_across(1, quarter).start()

    def body(i, carry):
        a, b, c = nth(2 * i), nth(2 * i + 1), nth(2 * i + 2)
        w_across(2 * i + 2, quarter).start()
        w_across(2 * i + 3, quarter).start()
        arrive_q(b)
        fused(b, a, 1)
        part_out(a).start()
        arrive_q(c)
        fused(c, b, 0)
        part_out(b).start()
        return carry

    lax.fori_loop(0, 3, body, 0)
    fused(0, order[6], 1)
    part_out(order[6]).start()
    fused(None, 0, 0)
    for so in range(2):
        got[0, so] = part[0, so]
    for n in range(RINGZ):
        w_across(n, partner).wait_recv()
    w_relay(partner).start()

    for dz in range(1, RINGZ):
        pltpu.make_async_remote_copy(
            src_ref=got.at[dz], dst_ref=got.at[dz], send_sem=p_r.at[dz],
            recv_sem=p_r.at[dz], device_id=plane(dz, 0), device_id_type=MESH,
        ).wait_recv()

    def merged(so):
        stats = [read_stats(got[dz, so, HEAD:, :].astype(F32)) for dz in range(RINGZ)]
        top = stats[0][0]
        for m, _ in stats[1:]:
            top = jnp.maximum(top, m)
        acc = jnp.zeros((HEAD, QH), F32)
        total = jnp.zeros((1, QH), F32)
        for dz, (m, l) in enumerate(stats):
            f = jnp.exp2(m - top)
            total = total + l * f
            acc = acc + got[dz, so, 0:HEAD, :].astype(F32) * f
        return acc, top, total

    acc, top, total = merged(1)
    ysend[0:HEAD, :] = acc.astype(BF)
    ysend[HEAD:, :] = write_stats(top, total)
    y_out = pltpu.make_async_remote_copy(
        src_ref=ysend, dst_ref=yget, send_sem=y_s, recv_sem=y_r,
        device_id=plane(0, 1), device_id_type=MESH,
    )
    y_out.start()
    acc, top, total = merged(0)
    y_out.wait_recv()
    m, l = read_stats(yget[HEAD:, :].astype(F32))
    new = jnp.maximum(top, m)
    f = jnp.exp2(top - new)
    g = jnp.exp2(m - new)
    total = total * f + l * g
    acc = acc * f + yget[0:HEAD, :].astype(F32) * g
    own = (acc / total).T.astype(BF)
    for h in range(HEADS):
        blk[:, h * HEAD : (h + 1) * HEAD] = own[h * ROWS : (h + 1) * ROWS, :]

    def attn_out(dz):
        back = (RINGZ - dz) % RINGZ
        return pltpu.make_async_remote_copy(
            src_ref=blk, dst_ref=attn.at[back], send_sem=a_s.at[dz],
            recv_sem=a_r.at[back], device_id=plane(dz, 0), device_id_type=MESH,
        )

    a_out = [attn_out(dz) for dz in (4, 3, 5, 2, 6, 1, 7)]
    for copy in a_out:
        copy.start()
    attn[0] = blk[...]

    in_swaps[5].wait_recv()
    w_relay((partner + 1 - 2 * core)).wait_recv()
    me = kvh * 4 + quarter

    def term_copy(n, j):
        return pltpu.make_async_remote_copy(
            src_ref=prod.at[j, n], dst_ref=terms.at[me], send_sem=t_s.at[j * RINGZ + n],
            recv_sem=t_r.at[me], device_id=group(j, (z + n) % RINGZ), device_id_type=MESH,
        )

    for dz in range(1, RINGZ):
        pltpu.make_async_remote_copy(
            src_ref=attn.at[dz], dst_ref=attn.at[dz], send_sem=a_r.at[dz],
            recv_sem=a_r.at[dz], device_id=plane(dz, 0), device_id_type=MESH,
        ).wait_recv()
    rows = jnp.concatenate([attn[n] for n in range(RINGZ)], axis=0)
    for j in range(4):
        res = jnp.dot(rows, wbuf[j], preferred_element_type=F32).astype(BF)
        for n in range(RINGZ):
            prod[j, n] = res[n * ROWS : (n + 1) * ROWS, :]
        for n in range(RINGZ):
            here = ((z + n) % RINGZ == kvh) & (quarter == j)

            @pl.when(here)
            def _():
                terms[me] = prod[j, n]

            @pl.when(jnp.logical_not(here))
            def _():
                term_copy(n, j).start()

    for idx in range(4 * RINGZ):

        @pl.when(idx != me)
        def _():
            pltpu.make_async_remote_copy(
                src_ref=terms.at[idx], dst_ref=terms.at[idx], send_sem=t_r.at[idx],
                recv_sem=t_r.at[idx], device_id=sibling, device_id_type=MESH,
            ).wait_recv()

    for j in range(4):
        res = terms[j].astype(F32)
        for k in range(1, RINGZ):
            res = res + terms[k * 4 + j].astype(F32)
        out_ref[j * ROWS : (j + 1) * ROWS, :] = res.astype(BF)

    for copy in q_out + out_swaps + a_out + [y_out, w_relay(partner)]:
        copy.wait_send()
    for n in range(RINGZ):
        w_across(n, quarter).wait_send()
    for dz in range(1, RINGZ):
        part_out(dz).wait_send()
    for j in range(4):
        for n in range(RINGZ):

            @pl.when(jnp.logical_not(((z + n) % RINGZ == kvh) & (quarter == j)))
            def _():
                term_copy(n, j).wait_send()


def local(q, k, v, ck, cv, length, branch, depth, w):
    hbm = pl.BlockSpec(memory_space=pl.ANY)
    smem = pl.BlockSpec(memory_space=pltpu.SMEM)
    dma = pltpu.SemaphoreType.DMA
    return pl.pallas_call(
        kernel,
        out_shape=jax.ShapeDtypeStruct((4 * ROWS, COLS), BF),
        in_specs=[hbm] * 5 + [smem] * 3 + [hbm],
        out_specs=pl.BlockSpec(memory_space=pltpu.VMEM),
        scratch_shapes=[
            pltpu.VMEM((RINGZ, 2, ROWS, QW), BF),
            pltpu.VMEM((KPOS, HEAD), BF),
            pltpu.VMEM((SHARD, HEAD), BF),
            pltpu.VMEM((BLK, VPOS), BF),
            pltpu.VMEM((128, HEAD), BF),
            pltpu.VMEM((2, 2, ROWS, QH), BF),
            pltpu.VMEM((4, HEADS * HEAD, COLS), BF),
            pltpu.VMEM((KPOS, 2 * QH), F32),
            pltpu.VMEM((KPOS, 2 * QH), F32),
            pltpu.VMEM((VPOS, 2 * QH), BF),
            pltpu.VMEM((8, 2 * QH), F32),
            pltpu.VMEM((8, 2 * QH), F32),
            pltpu.VMEM((RINGZ, 2, BLK, QH), BF),
            pltpu.VMEM((RINGZ, 2, BLK, QH), BF),
            pltpu.VMEM((BLK, QH), BF),
            pltpu.VMEM((BLK, QH), BF),
            pltpu.VMEM((ROWS, HEADS * HEAD), BF),
            pltpu.VMEM((RINGZ, ROWS, HEADS * HEAD), BF),
            pltpu.VMEM((4, RINGZ, ROWS, COLS), BF),
            pltpu.VMEM((4 * RINGZ, ROWS, COLS), BF),
            dma((6,)), dma((6,)), dma((6,)), dma((9,)), dma((9,)),
            dma((3 * RINGZ,)), dma((2 * RINGZ,)), dma((RINGZ,)), dma((RINGZ,)),
            dma(()), dma(()), dma((RINGZ,)), dma((RINGZ,)), dma((4 * RINGZ,)), dma((4 * RINGZ,)),
        ],
        compiler_params=pltpu.CompilerParams(
            collective_id=0, has_side_effects=True, vmem_limit_bytes=62 * 2**20
        ),
        cost_estimate=pl.CostEstimate(
            flops=9 * 10**9, bytes_accessed=2 * 2**20, transcendentals=2048 * 4224
        ),
    )(q, k, v, ck, cv, length, branch, depth, w)


def solution(mesh):
    in_specs = (
        P("ctx", "kvh"),
        P("ctx", "kvh"),
        P("ctx", "kvh"),
        P("ctx", "kvh"),
        P("ctx", "kvh"),
        P("ctx"),
        P("ctx"),
        P("ctx"),
        P("kvh", "ctx"),
    )
    return jax.shard_map(
        local, mesh=mesh, in_specs=in_specs, out_specs=P("kvh", "ctx"), check_vma=False
    )
```

```python
import math

import jax
import jax.numpy as jnp
from jax import lax
from jax.experimental import pallas as pl
from jax.experimental.pallas import tpu as pltpu
from jax.sharding import PartitionSpec as P

MESH = pl.DeviceIdType.MESH
BF = jnp.bfloat16
F32 = jnp.float32
HEAD = 128
HEADS = 8
ROWS = 16
RINGZ = 8
SHARD = 2048
PAIR = 2 * SHARD
CAND = 2 * ROWS
KPOS = PAIR + CAND
VPOS = PAIR + 128
QH = HEADS * ROWS
QW = HEADS * HEAD + 128
BLK = HEAD + 16
COLS = 256
NEG = -1e30
SCALE = math.log2(math.e) / math.sqrt(HEAD)
CQ = 256
CP = 1024
WROWS = HEADS * HEAD // RINGZ
W_EARLY = 2
FAR_FIRST = (4, 3, 5, 2, 6, 1, 7)
STEPS = ((0, 8), (6, 10), (1, 4), (9, 7), (11, 5), (13, 3), (15, 12), (2, 14))
ARRIVE = ((8, 6, 10), (4, 12), (2, 14, 1), (9, 7), (11, 5), (13, 3), (15,), ())
JOIN_EARLY = (4, 3)
JOIN_LATE = (5, 2, 6, 1, 7)


def split2(x):
    hi = x.astype(BF)
    lo = (x - hi.astype(F32)).astype(BF)
    return hi, lo


def kernel(
    q_hbm, k_hbm, v_hbm, ck_hbm, cv_hbm, len_hbm, branch_hbm, depth_hbm, w_hbm,
    out_ref,
    ints, qall, kbuf, vraw, vt, cvraw, cinfo, wbuf, sa, sb, pbuf, ma, mb, part, yget, zsend, got, blk, attn, prod, terms,
    loc, kv_s, kv_r, w_s, w_r, q_s, q_r, r_s, y_s, y_r, p_s, p_r, a_s, a_r, t_s, t_r,
):
    ctx = lax.axis_index("ctx")
    kvh = lax.axis_index("kvh")
    z = ctx // 4
    yh = (ctx // 2) % 2
    core = ctx % 2
    quarter = ctx % 4
    partner = (quarter + 2) % 4

    def plane(dz, so):
        zz = (z + dz) % RINGZ
        yy = (yh + so) % 2
        return (zz * 4 + yy * 2 + core, kvh)

    sibling = (ctx + 1 - 2 * core, kvh)

    def group(j, k):
        return (ctx - quarter + j, k)

    bar = pltpu.get_barrier_semaphore()
    peers = [plane(dz, 0) for dz in range(1, RINGZ)]
    peers += [group((quarter + j) % 4, kvh) for j in range(1, 4)]
    peers += [group(j, (kvh + dk) % RINGZ) for dk in range(1, RINGZ) for j in range(4)]
    for peer in peers:
        pl.semaphore_signal(bar, inc=1, device_id=peer, device_id_type=MESH)

    mine = pl.multiple_of(core * SHARD, SHARD)
    cmine = pl.multiple_of(PAIR + core * ROWS, ROWS)
    crow = pl.multiple_of(core * ROWS, ROWS)
    loads = [
        pltpu.make_async_copy(q_hbm, qall.at[0, :, pl.ds(0, HEADS * HEAD)], loc.at[0]),
        pltpu.make_async_copy(len_hbm, ints.at[0], loc.at[6]),
        pltpu.make_async_copy(branch_hbm, ints.at[1], loc.at[7]),
        pltpu.make_async_copy(depth_hbm, ints.at[2], loc.at[8]),
        pltpu.make_async_copy(k_hbm, kbuf.at[pl.ds(mine, SHARD)], loc.at[1]),
        pltpu.make_async_copy(ck_hbm, kbuf.at[pl.ds(cmine, ROWS)], loc.at[3]),
        pltpu.make_async_copy(cv_hbm, cvraw.at[pl.ds(crow, ROWS)], loc.at[4]),
        pltpu.make_async_copy(v_hbm, vraw, loc.at[2]),
        pltpu.make_async_copy(w_hbm, wbuf.at[quarter], loc.at[5]),
    ]
    for copy in loads:
        copy.start()
    for copy in loads[:4]:
        copy.wait()

    lane = lax.broadcasted_iota(jnp.int32, (ROWS, QH), 1)
    sub = lax.broadcasted_iota(jnp.int32, (ROWS, QH), 0)
    lane_row = lane % ROWS
    meta = jnp.zeros((ROWS, QH), jnp.int32)
    cb = jnp.zeros((ROWS, QH), jnp.int32)
    cd = jnp.zeros((ROWS, QH), jnp.int32)
    for i in range(ROWS):
        n = ints[0, i]
        b = ints[1, i]
        d = ints[2, i]
        high = n // 256
        col = jnp.where(
            sub == 0, high, jnp.where(sub == 1, n - high * 256, jnp.where(sub == 2, b, d))
        )
        meta = jnp.where(lane_row == i, col, meta)
        cb = jnp.where(sub == i, b, cb)
        cd = jnp.where(sub == i, d, cd)
    qall[0, :, HEADS * HEAD :] = meta.astype(F32).astype(BF)
    cinfo[core, 0] = cb.astype(F32).astype(BF)
    cinfo[core, 1] = cd.astype(F32).astype(BF)
    pbuf[KPOS:, :] = jnp.zeros((VPOS - KPOS, 2 * QH), BF)
    vt[HEAD:, :] = jnp.ones((BLK - HEAD, VPOS), BF)
    cvraw[CAND:, :] = jnp.zeros((128 - CAND, HEAD), BF)

    def block_to(src, dst, send, recv, peer):
        return pltpu.make_async_remote_copy(
            src_ref=src, dst_ref=dst, send_sem=send, recv_sem=recv, device_id=peer, device_id_type=MESH
        )

    def arrived(dst, recv):
        block_to(dst, dst, recv, recv, sibling).wait_recv()

    across = plane(0, 1)

    def query_z(dz):
        back = (RINGZ - dz) % RINGZ
        return block_to(
            qall.at[0], qall.at[2 * back], q_s.at[dz], q_r.at[2 * back], plane(dz, 0)
        )

    def query_y(dz):
        return block_to(
            qall.at[2 * dz], qall.at[2 * dz + 1], r_s.at[dz], q_r.at[2 * dz + 1], across
        )

    def part_y(dz):
        return block_to(part.at[2 * dz + 1], yget.at[dz], y_s.at[dz], y_r.at[dz], across)

    def part_z(dz):
        back = (RINGZ - dz) % RINGZ
        return block_to(zsend.at[dz], got.at[back], p_s.at[dz], p_r.at[back], plane(dz, 0))

    def w_across(n, slab):
        rows = pl.ds(n * WROWS, WROWS)
        return block_to(
            wbuf.at[slab, rows], wbuf.at[slab, rows], w_s.at[n], w_r.at[n], across
        )

    def w_relay(slab):
        return block_to(wbuf.at[slab], wbuf.at[slab], w_s.at[RINGZ], w_r.at[RINGZ], sibling)

    def swap(n, ref):
        return block_to(ref, ref, kv_s.at[n], kv_r.at[n], sibling)

    def swaps(side):
        base = pl.multiple_of(side * SHARD, SHARD)
        cbase = pl.multiple_of(PAIR + side * ROWS, ROWS)
        rbase = pl.multiple_of(side * ROWS, ROWS)
        return [
            swap(0, kbuf.at[pl.ds(base, SHARD)]),
            swap(1, kbuf.at[pl.ds(cbase, ROWS)]),
            swap(2, cvraw.at[pl.ds(rbase, ROWS)]),
            swap(3, cinfo.at[side]),
            swap(4, vt.at[pl.ds(0, HEAD), pl.ds(base, SHARD)]),
            swap(5, wbuf.at[quarter - core + side]),
        ]

    pl.semaphore_wait(bar, len(peers))
    query_y(0).start()
    for dz in FAR_FIRST:
        query_z(dz).start()
    out_swaps = swaps(core)
    in_swaps = swaps(1 - core)
    for copy in loads[4:7]:
        copy.wait()
    for copy in out_swaps[:4]:
        copy.start()
    loads[7].wait()
    for j in range(0, SHARD, 128):
        vt[0:HEAD, pl.ds(pl.multiple_of(mine + j, 128), 128)] = vraw[j : j + 128, :].T
    out_swaps[4].start()
    loads[8].wait()
    out_swaps[5].start()
    for n in range(W_EARLY):
        w_across(n, quarter).start()

    base = (ctx - core) * SHARD
    pos_sub = lax.broadcasted_iota(jnp.int32, (CQ, QH), 0)

    def read_stats(st):
        return st[0:1] + st[1:2] + st[2:3], st[3:4] + st[4:5]

    def write_stats(m, total):
        m_hi = m.astype(BF)
        m_mid, m_lo = split2(m - m_hi.astype(F32))
        l_hi, l_lo = split2(total)
        row = lax.broadcasted_iota(jnp.int32, (BLK - HEAD, m.shape[1]), 0)
        stats = jnp.zeros((BLK - HEAD, m.shape[1]), F32)
        for n, x in enumerate((m_hi, m_mid, m_lo, l_hi, l_lo)):
            stats = jnp.where(row == n, x.astype(F32), stats)
        return stats.astype(BF)

    def load_q(pair):
        parts = []
        infos = []
        for slot in pair:
            for h in range(HEADS):
                parts.append(qall[slot, :, h * HEAD : (h + 1) * HEAD])
            infos.append(qall[slot, :, HEADS * HEAD :].astype(F32))
        q = jnp.concatenate(parts, axis=0).astype(F32) * SCALE
        hi, lo = split2(q)
        lens = [(f[0:1] * 256.0 + f[1:2]).astype(jnp.int32) - base for f in infos]
        return jnp.concatenate([hi, lo], axis=1), lens, infos

    def score(q, pos, width):
        k = kbuf[pos : pos + width, :]
        return lax.dot_general(
            jnp.concatenate([k, k], axis=1), q, (((1,), (1,)), ((), ())),
            preferred_element_type=F32,
        )

    def fused(new, old, parity):
        s_new, s_old = (sa, sb) if parity == 0 else (sb, sa)
        m_new, m_old = (ma, mb) if parity == 0 else (mb, ma)
        if new is not None:
            q, lens, infos = load_q(new)
            top = jnp.full((8, 2 * QH), NEG, F32)
            s = score(q, PAIR, CAND)
            cbr = jnp.concatenate([cinfo[0, 0], cinfo[1, 0]], axis=0).astype(F32)
            cde = jnp.concatenate([cinfo[0, 1], cinfo[1, 1]], axis=0).astype(F32)
            s = jnp.concatenate(
                [
                    jnp.where(
                        (cbr == f[2:3]) & (cde <= f[3:4]), s[:, n * QH : (n + 1) * QH], NEG
                    )
                    for n, f in enumerate(infos)
                ],
                axis=1,
            )
            s_new[PAIR:KPOS, :] = s
            for j in range(0, CAND, 8):
                top = jnp.maximum(top, s[j : j + 8, :])
        if old is not None:
            m = m_old[0:1, :]
            acc = None
            start = 0
        for pos in range(0, PAIR, CQ):
            if new is not None:
                s = score(q, pos, CQ)
                s = jnp.concatenate(
                    [
                        jnp.where(pos_sub < n - pos, s[:, j * QH : (j + 1) * QH], NEG)
                        for j, n in enumerate(lens)
                    ],
                    axis=1,
                )
                s_new[pos : pos + CQ, :] = s
                for j in range(0, CQ, 8):
                    top = jnp.maximum(top, s[j : j + 8, :])
            if old is not None:
                pbuf[pos : pos + CQ, :] = jnp.exp2(s_old[pos : pos + CQ, :] - m).astype(BF)
                end = pos + CQ
                if end == PAIR:
                    pbuf[PAIR:KPOS, :] = jnp.exp2(s_old[PAIR:KPOS, :] - m).astype(BF)
                    end = VPOS
                if end - start >= CP:
                    term = jnp.dot(
                        vt[:, start:end], pbuf[start:end, :], preferred_element_type=F32
                    )
                    acc = term if acc is None else acc + term
                    start = end
        if old is not None:
            total = acc[HEAD : HEAD + 1]
            stats = write_stats(m, total)
            for n, slot in enumerate(old):
                lanes = slice(n * QH, (n + 1) * QH)
                part[slot, 0:HEAD, :] = acc[0:HEAD, lanes].astype(BF)
                part[slot, HEAD:, :] = stats[:, lanes]
        if new is not None:
            m_new[...] = jnp.broadcast_to(jnp.max(top, axis=0, keepdims=True), (8, 2 * QH))

    def nth(t):
        pair = []
        for side in range(2):
            slot = jnp.int32(STEPS[0][side])
            for n in range(1, RINGZ):
                slot = jnp.where(t == n, STEPS[n][side], slot)
            pair.append(slot)
        return pair

    def ready(t):
        for slot in ARRIVE[t]:
            arrived(qall.at[slot], q_r.at[slot])
            if slot % 2 == 0:
                query_y(slot // 2).start()

    def finished(t):
        for slot in STEPS[t]:
            if slot % 2:
                part_y(slot // 2).start()

    def at(i, fn, steps):
        for n, t in enumerate(steps):
            pl.when(i == n)(lambda t=t: fn(t))

    for n in range(4):
        in_swaps[n].wait_recv()
    ready(0)
    fused(STEPS[0], None, 0)
    in_swaps[4].wait_recv()
    vt[0:HEAD, PAIR:] = cvraw[...].T

    def body(i, carry):
        a, b, c = nth(2 * i), nth(2 * i + 1), nth(2 * i + 2)
        at(i, ready, (1, 3, 5))
        fused(b, a, 1)
        at(i, finished, (0, 2, 4))
        at(i, ready, (2, 4, 6))
        fused(c, b, 0)
        at(i, finished, (1, 3, 5))
        return carry

    lax.fori_loop(0, 3, body, 0)
    ready(7)
    fused(STEPS[7], STEPS[6], 1)
    finished(6)
    for n in range(W_EARLY, RINGZ):
        w_across(n, quarter).start()

    def merge(stats, accs):
        top = stats[0][0]
        for m, _ in stats[1:]:
            top = jnp.maximum(top, m)
        acc = total = None
        for (m, l), x in zip(stats, accs):
            f = jnp.exp2(m - top)
            total = l * f if total is None else total + l * f
            term = x.astype(F32) * f
            acc = term if acc is None else acc + term
        return acc, top, total

    def join(dz, dst):
        arrived(yget.at[dz], y_r.at[dz])
        refs = (part.at[2 * dz], yget.at[dz])
        acc, top, total = merge(
            [read_stats(ref[HEAD:, :].astype(F32)) for ref in refs], [ref[0:HEAD, :] for ref in refs]
        )
        dst[0:HEAD, :] = acc.astype(BF)
        dst[HEAD:, :] = write_stats(top, total)

    for dz in JOIN_EARLY:
        join(dz, zsend.at[dz])
        part_z(dz).start()
    fused(None, STEPS[7], 0)
    for dz in JOIN_LATE:
        join(dz, zsend.at[dz])
        part_z(dz).start()
    join(0, got.at[0])

    for dz in range(1, RINGZ):
        arrived(got.at[dz], p_r.at[dz])
    acc, top, total = merge(
        [read_stats(got[dz, HEAD:, :].astype(F32)) for dz in range(RINGZ)],
        [got[dz, 0:HEAD, :] for dz in range(RINGZ)],
    )
    own = (acc / total).T.astype(BF)
    for h in range(HEADS):
        blk[:, h * HEAD : (h + 1) * HEAD] = own[h * ROWS : (h + 1) * ROWS, :]

    def attn_out(dz):
        back = (RINGZ - dz) % RINGZ
        return block_to(blk, attn.at[back], a_s.at[dz], a_r.at[back], plane(dz, 0))

    for dz in FAR_FIRST:
        attn_out(dz).start()
    attn[0] = blk[...]
    for n in range(RINGZ):
        w_across(n, partner).wait_recv()
    w_relay(partner).start()

    in_swaps[5].wait_recv()
    w_relay((partner + 1 - 2 * core)).wait_recv()
    me = kvh * 4 + quarter

    def term_copy(n, j):
        return block_to(
            prod.at[j, n], terms.at[me], t_s.at[j * RINGZ + n], t_r.at[me],
            group(j, (z + n) % RINGZ),
        )

    for dz in range(1, RINGZ):
        arrived(attn.at[dz], a_r.at[dz])
    rows = jnp.concatenate([attn[n] for n in range(RINGZ)], axis=0)
    for j in range(4):
        res = jnp.dot(rows, wbuf[j], preferred_element_type=F32).astype(BF)
        for n in range(RINGZ):
            prod[j, n] = res[n * ROWS : (n + 1) * ROWS, :]
        for n in range(RINGZ):
            here = ((z + n) % RINGZ == kvh) & (quarter == j)

            @pl.when(here)
            def _():
                terms[me] = prod[j, n]

            @pl.when(jnp.logical_not(here))
            def _():
                term_copy(n, j).start()

    for idx in range(4 * RINGZ):

        @pl.when(idx != me)
        def _():
            arrived(terms.at[idx], t_r.at[idx])

    for j in range(4):
        res = terms[j].astype(F32)
        for k in range(1, RINGZ):
            res = res + terms[k * 4 + j].astype(F32)
        out_ref[j * ROWS : (j + 1) * ROWS, :] = res.astype(BF)

    for copy in out_swaps + [w_relay(partner)]:
        copy.wait_send()
    for dz in range(RINGZ):
        query_y(dz).wait_send()
        part_y(dz).wait_send()
        w_across(dz, quarter).wait_send()
        if dz:
            query_z(dz).wait_send()
            part_z(dz).wait_send()
            attn_out(dz).wait_send()
    for j in range(4):
        for n in range(RINGZ):

            @pl.when(jnp.logical_not(((z + n) % RINGZ == kvh) & (quarter == j)))
            def _():
                term_copy(n, j).wait_send()


def local(q, k, v, ck, cv, length, branch, depth, w):
    hbm = pl.BlockSpec(memory_space=pl.ANY)
    dma = pltpu.SemaphoreType.DMA
    return pl.pallas_call(
        kernel,
        out_shape=jax.ShapeDtypeStruct((4 * ROWS, COLS), BF),
        in_specs=[hbm] * 9,
        out_specs=pl.BlockSpec(memory_space=pltpu.VMEM),
        scratch_shapes=[
            pltpu.SMEM((3, ROWS), jnp.int32),
            pltpu.VMEM((2 * RINGZ, ROWS, QW), BF),
            pltpu.VMEM((KPOS, HEAD), BF),
            pltpu.VMEM((SHARD, HEAD), BF),
            pltpu.VMEM((BLK, VPOS), BF),
            pltpu.VMEM((128, HEAD), BF),
            pltpu.VMEM((2, 2, ROWS, QH), BF),
            pltpu.VMEM((4, HEADS * HEAD, COLS), BF),
            pltpu.VMEM((KPOS, 2 * QH), F32),
            pltpu.VMEM((KPOS, 2 * QH), F32),
            pltpu.VMEM((VPOS, 2 * QH), BF),
            pltpu.VMEM((8, 2 * QH), F32),
            pltpu.VMEM((8, 2 * QH), F32),
            pltpu.VMEM((2 * RINGZ, BLK, QH), BF),
            pltpu.VMEM((RINGZ, BLK, QH), BF),
            pltpu.VMEM((RINGZ, BLK, QH), BF),
            pltpu.VMEM((RINGZ, BLK, QH), BF),
            pltpu.VMEM((ROWS, HEADS * HEAD), BF),
            pltpu.VMEM((RINGZ, ROWS, HEADS * HEAD), BF),
            pltpu.VMEM((4, RINGZ, ROWS, COLS), BF),
            pltpu.VMEM((4 * RINGZ, ROWS, COLS), BF),
            dma((9,)), dma((6,)), dma((6,)), dma((9,)), dma((9,)),
            dma((RINGZ,)), dma((2 * RINGZ,)), dma((RINGZ,)),
            dma((RINGZ,)), dma((RINGZ,)), dma((RINGZ,)), dma((RINGZ,)),
            dma((RINGZ,)), dma((RINGZ,)), dma((4 * RINGZ,)), dma((4 * RINGZ,)),
        ],
        compiler_params=pltpu.CompilerParams(
            collective_id=0, has_side_effects=True, vmem_limit_bytes=62 * 2**20
        ),
        cost_estimate=pl.CostEstimate(
            flops=9 * 10**9, bytes_accessed=2 * 2**20, transcendentals=2048 * 4224
        ),
    )(q, k, v, ck, cv, length, branch, depth, w)


def solution(mesh):
    in_specs = (
        P("ctx", "kvh"),
        P("ctx", "kvh"),
        P("ctx", "kvh"),
        P("ctx", "kvh"),
        P("ctx", "kvh"),
        P("ctx"),
        P("ctx"),
        P("ctx"),
        P("kvh", "ctx"),
    )
    return jax.shard_map(
        local, mesh=mesh, in_specs=in_specs, out_specs=P("kvh", "ctx"), check_vma=False
    )
```

```python
import math

import jax
import jax.numpy as jnp
from jax import lax
from jax.experimental import pallas as pl
from jax.experimental.pallas import tpu as pltpu
from jax.sharding import PartitionSpec as P

MESH = pl.DeviceIdType.MESH
BF = jnp.bfloat16
F32 = jnp.float32
HEAD = 128
HEADS = 8
ROWS = 16
RINGZ = 8
SHARD = 2048
PAIR = 2 * SHARD
CAND = 2 * ROWS
KPOS = PAIR + CAND
VPOS = PAIR + 128
QH = HEADS * ROWS
QW = HEADS * HEAD + 128
BLK = HEAD + 16
COLS = 256
NEG = -1e30
SCALE = math.log2(math.e) / math.sqrt(HEAD)
CQ = 256
CP = 1024
WROWS = HEADS * HEAD // RINGZ
FAR_FIRST = (4, 3, 5, 2, 6, 1, 7)
QUERY_ORDER = ((1, 0), (7, 0), (0, 1), (2, 0), (6, 0), (3, 0), (5, 0), (4, 0))
JOINED = ()
JOIN_EARLY = 0
STEPS = ((0, 2), (14, 4), (1, 12), (6, 10), (3, 15), (5, 13), (7, 11), (9, 8))
ARRIVE = ((2, 14), (4, 12), (1, 6, 10), (8,), (3, 15), (5, 13), (7, 11), (9,))
W_AT = (0, 0, 0, 1, 2, 3, 4, 5, 8)


def split2(x):
    hi = x.astype(BF)
    lo = (x - hi.astype(F32)).astype(BF)
    return hi, lo


def kernel(
    q_hbm, k_hbm, v_hbm, ck_hbm, cv_hbm, len_hbm, branch_hbm, depth_hbm, w_hbm,
    terms,
    ints, qall, kbuf, vraw, vt, cvraw, cinfo, wbuf, sa, sb, pbuf, ma, mb, part, yget, zsend, got, gotd, blk, attn, prod,
    loc, kv_s, kv_r, w_s, w_r, q_s, q_r, r_s, y_s, y_r, p_s, p_r, d_r, a_s, a_r, t_s, t_r,
):
    ctx = lax.axis_index("ctx")
    kvh = lax.axis_index("kvh")
    z = ctx // 4
    yh = (ctx // 2) % 2
    core = ctx % 2
    quarter = ctx % 4
    partner = (quarter + 2) % 4

    def plane(dz, so):
        zz = (z + dz) % RINGZ
        yy = (yh + so) % 2
        return (zz * 4 + yy * 2 + core, kvh)

    sibling = (ctx + 1 - 2 * core, kvh)

    def group(j, k):
        return (ctx - quarter + j, k)

    bar = pltpu.get_barrier_semaphore()
    peers = [plane(dz, so) for dz in range(1, RINGZ) for so in range(2)]
    peers += [group((quarter + j) % 4, kvh) for j in range(1, 4)]
    peers += [group(j, (kvh + dk) % RINGZ) for dk in range(1, RINGZ) for j in range(4)]
    for peer in peers:
        pl.semaphore_signal(bar, inc=1, device_id=peer, device_id_type=MESH)

    mine = pl.multiple_of(core * SHARD, SHARD)
    cmine = pl.multiple_of(PAIR + core * ROWS, ROWS)
    crow = pl.multiple_of(core * ROWS, ROWS)
    loads = [
        pltpu.make_async_copy(q_hbm, qall.at[0, :, pl.ds(0, HEADS * HEAD)], loc.at[0]),
        pltpu.make_async_copy(len_hbm, ints.at[0], loc.at[6]),
        pltpu.make_async_copy(branch_hbm, ints.at[1], loc.at[7]),
        pltpu.make_async_copy(depth_hbm, ints.at[2], loc.at[8]),
        pltpu.make_async_copy(k_hbm, kbuf.at[pl.ds(mine, SHARD)], loc.at[1]),
        pltpu.make_async_copy(ck_hbm, kbuf.at[pl.ds(cmine, ROWS)], loc.at[3]),
        pltpu.make_async_copy(cv_hbm, cvraw.at[pl.ds(crow, ROWS)], loc.at[4]),
        pltpu.make_async_copy(v_hbm, vraw, loc.at[2]),
        pltpu.make_async_copy(w_hbm, wbuf.at[quarter], loc.at[5]),
    ]
    for copy in loads:
        copy.start()
    for copy in loads[:4]:
        copy.wait()

    lane = lax.broadcasted_iota(jnp.int32, (ROWS, QH), 1)
    sub = lax.broadcasted_iota(jnp.int32, (ROWS, QH), 0)
    lane_row = lane % ROWS
    meta = jnp.zeros((ROWS, QH), jnp.int32)
    cb = jnp.zeros((ROWS, QH), jnp.int32)
    cd = jnp.zeros((ROWS, QH), jnp.int32)
    for i in range(ROWS):
        n = ints[0, i]
        b = ints[1, i]
        d = ints[2, i]
        high = n // 256
        col = jnp.where(
            sub == 0, high, jnp.where(sub == 1, n - high * 256, jnp.where(sub == 2, b, d))
        )
        meta = jnp.where(lane_row == i, col, meta)
        cb = jnp.where(sub == i, b, cb)
        cd = jnp.where(sub == i, d, cd)
    qall[0, :, HEADS * HEAD :] = meta.astype(F32).astype(BF)
    cinfo[core, 0] = cb.astype(F32).astype(BF)
    cinfo[core, 1] = cd.astype(F32).astype(BF)
    pbuf[KPOS:, :] = jnp.zeros((VPOS - KPOS, 2 * QH), BF)
    vt[HEAD:, :] = jnp.ones((BLK - HEAD, VPOS), BF)
    cvraw[CAND:, :] = jnp.zeros((128 - CAND, HEAD), BF)

    def block_to(src, dst, send, recv, peer):
        return pltpu.make_async_remote_copy(
            src_ref=src, dst_ref=dst, send_sem=send, recv_sem=recv, device_id=peer, device_id_type=MESH
        )

    def arrived(dst, recv):
        block_to(dst, dst, recv, recv, sibling).wait_recv()

    across = plane(0, 1)

    def query_z(dz):
        back = (RINGZ - dz) % RINGZ
        return block_to(
            qall.at[0], qall.at[2 * back], q_s.at[dz], q_r.at[2 * back], plane(dz, 0)
        )

    def query_d(dz):
        back = (RINGZ - dz) % RINGZ
        return block_to(
            qall.at[0], qall.at[2 * back + 1], r_s.at[dz], q_r.at[2 * back + 1], plane(dz, 1)
        )

    def query_y(dz):
        return block_to(
            qall.at[2 * dz], qall.at[2 * dz + 1], r_s.at[dz], q_r.at[2 * dz + 1], across
        )

    def part_y(dz):
        return block_to(part.at[2 * dz + 1], yget.at[dz], y_s.at[dz], y_r.at[dz], across)

    def part_z(dz):
        back = (RINGZ - dz) % RINGZ
        src = zsend.at[dz] if dz in JOINED else part.at[2 * dz]
        return block_to(src, got.at[back], p_s.at[dz], p_r.at[back], plane(dz, 0))

    def part_d(dz):
        back = (RINGZ - dz) % RINGZ
        return block_to(
            part.at[2 * dz + 1], gotd.at[back], y_s.at[dz], d_r.at[back], plane(dz, 1)
        )

    def w_across(n, slab):
        rows = pl.ds(n * WROWS, WROWS)
        return block_to(
            wbuf.at[slab, rows], wbuf.at[slab, rows], w_s.at[n], w_r.at[n], across
        )

    def w_relay(slab):
        return block_to(wbuf.at[slab], wbuf.at[slab], w_s.at[RINGZ], w_r.at[RINGZ], sibling)

    def swap(n, ref):
        return block_to(ref, ref, kv_s.at[n], kv_r.at[n], sibling)

    def swaps(side):
        base = pl.multiple_of(side * SHARD, SHARD)
        cbase = pl.multiple_of(PAIR + side * ROWS, ROWS)
        rbase = pl.multiple_of(side * ROWS, ROWS)
        return [
            swap(0, kbuf.at[pl.ds(base, SHARD)]),
            swap(1, kbuf.at[pl.ds(cbase, ROWS)]),
            swap(2, cvraw.at[pl.ds(rbase, ROWS)]),
            swap(3, cinfo.at[side]),
            swap(4, vt.at[pl.ds(0, HEAD), pl.ds(base, SHARD)]),
            swap(5, wbuf.at[quarter - core + side]),
        ]

    pl.semaphore_wait(bar, len(peers))
    for dz, so in QUERY_ORDER:
        (query_d(dz) if dz and so else query_y(0) if so else query_z(dz)).start()
    out_swaps = swaps(core)
    in_swaps = swaps(1 - core)
    for copy in loads[4:7]:
        copy.wait()
    for copy in out_swaps[:4]:
        copy.start()
    loads[7].wait()
    for j in range(0, SHARD, 128):
        vt[0:HEAD, pl.ds(pl.multiple_of(mine + j, 128), 128)] = vraw[j : j + 128, :].T
    out_swaps[4].start()
    loads[8].wait()
    out_swaps[5].start()
    base = (ctx - core) * SHARD
    pos_sub = lax.broadcasted_iota(jnp.int32, (CQ, QH), 0)

    def read_stats(st):
        return st[0:1] + st[1:2] + st[2:3], st[3:4] + st[4:5]

    def write_stats(m, total):
        m_hi = m.astype(BF)
        m_mid, m_lo = split2(m - m_hi.astype(F32))
        l_hi, l_lo = split2(total)
        row = lax.broadcasted_iota(jnp.int32, (BLK - HEAD, m.shape[1]), 0)
        stats = jnp.zeros((BLK - HEAD, m.shape[1]), F32)
        for n, x in enumerate((m_hi, m_mid, m_lo, l_hi, l_lo)):
            stats = jnp.where(row == n, x.astype(F32), stats)
        return stats.astype(BF)

    def load_q(pair):
        parts = []
        infos = []
        for slot in pair:
            for h in range(HEADS):
                parts.append(qall[slot, :, h * HEAD : (h + 1) * HEAD])
            infos.append(qall[slot, :, HEADS * HEAD :].astype(F32))
        q = jnp.concatenate(parts, axis=0).astype(F32) * SCALE
        hi, lo = split2(q)
        lens = [(f[0:1] * 256.0 + f[1:2]).astype(jnp.int32) - base for f in infos]
        return jnp.concatenate([hi, lo], axis=1), lens, infos

    def score(q, pos, width):
        k = kbuf[pos : pos + width, :]
        return lax.dot_general(
            jnp.concatenate([k, k], axis=1), q, (((1,), (1,)), ((), ())),
            preferred_element_type=F32,
        )

    def fused(new, old, parity):
        s_new, s_old = (sa, sb) if parity == 0 else (sb, sa)
        m_new, m_old = (ma, mb) if parity == 0 else (mb, ma)
        if new is not None:
            q, lens, infos = load_q(new)
            top = jnp.full((8, 2 * QH), NEG, F32)
            s = score(q, PAIR, CAND)
            cbr = jnp.concatenate([cinfo[0, 0], cinfo[1, 0]], axis=0).astype(F32)
            cde = jnp.concatenate([cinfo[0, 1], cinfo[1, 1]], axis=0).astype(F32)
            s = jnp.concatenate(
                [
                    jnp.where(
                        (cbr == f[2:3]) & (cde <= f[3:4]), s[:, n * QH : (n + 1) * QH], NEG
                    )
                    for n, f in enumerate(infos)
                ],
                axis=1,
            )
            s_new[PAIR:KPOS, :] = s
            for j in range(0, CAND, 8):
                top = jnp.maximum(top, s[j : j + 8, :])
        if old is not None:
            m = m_old[0:1, :]
            acc = None
            start = 0
        for pos in range(0, PAIR, CQ):
            if new is not None:
                s = score(q, pos, CQ)
                s = jnp.concatenate(
                    [
                        jnp.where(pos_sub < n - pos, s[:, j * QH : (j + 1) * QH], NEG)
                        for j, n in enumerate(lens)
                    ],
                    axis=1,
                )
                s_new[pos : pos + CQ, :] = s
                for j in range(0, CQ, 8):
                    top = jnp.maximum(top, s[j : j + 8, :])
            if old is not None:
                pbuf[pos : pos + CQ, :] = jnp.exp2(s_old[pos : pos + CQ, :] - m).astype(BF)
                end = pos + CQ
                if end == PAIR:
                    pbuf[PAIR:KPOS, :] = jnp.exp2(s_old[PAIR:KPOS, :] - m).astype(BF)
                    end = VPOS
                if end - start >= CP:
                    term = jnp.dot(
                        vt[:, start:end], pbuf[start:end, :], preferred_element_type=F32
                    )
                    acc = term if acc is None else acc + term
                    start = end
        if old is not None:
            total = acc[HEAD : HEAD + 1]
            stats = write_stats(m, total)
            for n, slot in enumerate(old):
                lanes = slice(n * QH, (n + 1) * QH)
                part[slot, 0:HEAD, :] = acc[0:HEAD, lanes].astype(BF)
                part[slot, HEAD:, :] = stats[:, lanes]
        if new is not None:
            m_new[...] = jnp.broadcast_to(jnp.max(top, axis=0, keepdims=True), (8, 2 * QH))

    def nth(t):
        pair = []
        for side in range(2):
            slot = jnp.int32(STEPS[0][side])
            for n in range(1, RINGZ):
                slot = jnp.where(t == n, STEPS[n][side], slot)
            pair.append(slot)
        return pair

    def ready(t):
        for slot in ARRIVE[t]:
            arrived(qall.at[slot], q_r.at[slot])
            if slot % 2 == 0 and (slot // 2, 1) not in QUERY_ORDER:
                query_y(slot // 2).start()

    def finished(t):
        for slot in STEPS[t]:
            dz = slot // 2
            if slot % 2:
                (part_y if dz in JOINED or dz == 0 else part_d)(dz).start()
            elif dz and dz not in JOINED:
                part_z(dz).start()
        for n in range(W_AT[t], W_AT[t + 1]):
            w_across(n, quarter).start()

    def at(i, fn, steps):
        for n, t in enumerate(steps):
            pl.when(i == n)(lambda t=t: fn(t))

    for n in range(4):
        in_swaps[n].wait_recv()
    ready(0)
    fused(STEPS[0], None, 0)
    in_swaps[4].wait_recv()
    vt[0:HEAD, PAIR:] = cvraw[...].T

    def body(i, carry):
        a, b, c = nth(2 * i), nth(2 * i + 1), nth(2 * i + 2)
        at(i, ready, (1, 3, 5))
        fused(b, a, 1)
        at(i, finished, (0, 2, 4))
        at(i, ready, (2, 4, 6))
        fused(c, b, 0)
        at(i, finished, (1, 3, 5))
        return carry

    lax.fori_loop(0, 3, body, 0)
    ready(7)
    fused(STEPS[7], STEPS[6], 1)
    finished(6)
    def merge(stats, accs):
        top = stats[0][0]
        for m, _ in stats[1:]:
            top = jnp.maximum(top, m)
        acc = total = None
        for (m, l), x in zip(stats, accs):
            f = jnp.exp2(m - top)
            total = l * f if total is None else total + l * f
            term = x.astype(F32) * f
            acc = term if acc is None else acc + term
        return acc, top, total

    def join(dz, dst):
        arrived(yget.at[dz], y_r.at[dz])
        refs = (part.at[2 * dz], yget.at[dz])
        acc, top, total = merge(
            [read_stats(ref[HEAD:, :].astype(F32)) for ref in refs], [ref[0:HEAD, :] for ref in refs]
        )
        dst[0:HEAD, :] = acc.astype(BF)
        dst[HEAD:, :] = write_stats(top, total)

    for dz in JOINED[:JOIN_EARLY]:
        join(dz, zsend.at[dz])
        part_z(dz).start()
    fused(None, STEPS[7], 0)
    finished(7)
    for dz in JOINED[JOIN_EARLY:]:
        join(dz, zsend.at[dz])
        part_z(dz).start()
    join(0, got.at[0])

    for dz in range(1, RINGZ):
        arrived(got.at[dz], p_r.at[dz])
    singles = [dz for dz in range(1, RINGZ) if dz not in JOINED]
    for dz in singles:
        back = RINGZ - dz
        arrived(gotd.at[back], d_r.at[back])
    refs = [got.at[dz] for dz in range(RINGZ)] + [gotd.at[(RINGZ - dz) % RINGZ] for dz in singles]
    acc, top, total = merge(
        [read_stats(ref[HEAD:, :].astype(F32)) for ref in refs], [ref[0:HEAD, :] for ref in refs]
    )
    own = (acc / total).T.astype(BF)
    for h in range(HEADS):
        blk[:, h * HEAD : (h + 1) * HEAD] = own[h * ROWS : (h + 1) * ROWS, :]

    def attn_out(dz):
        back = (RINGZ - dz) % RINGZ
        return block_to(blk, attn.at[back], a_s.at[dz], a_r.at[back], plane(dz, 0))

    for dz in FAR_FIRST:
        attn_out(dz).start()
    attn[0] = blk[...]
    for n in range(RINGZ):
        w_across(n, partner).wait_recv()
    w_relay(partner).start()

    in_swaps[5].wait_recv()
    w_relay((partner + 1 - 2 * core)).wait_recv()
    me = kvh * 4 + quarter

    def term_copy(i, n):
        return block_to(
            prod.at[i, n], terms.at[me], t_s.at[i * RINGZ + n], t_r.at[me],
            group((quarter + i) % 4, (z + n) % RINGZ),
        )

    def own_term(n):
        return pltpu.make_async_copy(prod.at[0, n], terms.at[me], t_s.at[n])

    for dz in range(1, RINGZ):
        arrived(attn.at[dz], a_r.at[dz])
    rows = jnp.concatenate([attn[n] for n in range(RINGZ)], axis=0)
    for i in (2, 3, 1, 0):
        j = (quarter + i) % 4
        res = jnp.dot(rows, wbuf[j], preferred_element_type=F32).astype(BF)
        for n in range(RINGZ):
            prod[i, n] = res[n * ROWS : (n + 1) * ROWS, :]
        for n in range(RINGZ):
            if i:
                term_copy(i, n).start()
            else:
                here = (z + n) % RINGZ == kvh

                @pl.when(here)
                def _():
                    own_term(n).start()

                @pl.when(jnp.logical_not(here))
                def _():
                    term_copy(i, n).start()

    for copy in out_swaps + [w_relay(partner)]:
        copy.wait_send()
    for dz in range(RINGZ):
        (query_d if dz and (dz, 1) in QUERY_ORDER else query_y)(dz).wait_send()
        (part_y if dz in JOINED or dz == 0 else part_d)(dz).wait_send()
        w_across(dz, quarter).wait_send()
        if dz:
            query_z(dz).wait_send()
            part_z(dz).wait_send()
            attn_out(dz).wait_send()
    for i in range(4):
        for n in range(RINGZ):
            if i:
                term_copy(i, n).wait_send()
            else:
                here = (z + n) % RINGZ == kvh

                @pl.when(here)
                def _():
                    own_term(n).wait()

                @pl.when(jnp.logical_not(here))
                def _():
                    term_copy(i, n).wait_send()

    for idx in range(4 * RINGZ):

        @pl.when(idx != me)
        def _():
            arrived(terms.at[idx], t_r.at[idx])


def local(q, k, v, ck, cv, length, branch, depth, w):
    hbm = pl.BlockSpec(memory_space=pl.ANY)
    dma = pltpu.SemaphoreType.DMA
    terms = pl.pallas_call(
        kernel,
        out_shape=jax.ShapeDtypeStruct((4 * RINGZ, ROWS, COLS), BF),
        in_specs=[hbm] * 9,
        out_specs=hbm,
        scratch_shapes=[
            pltpu.SMEM((3, ROWS), jnp.int32),
            pltpu.VMEM((2 * RINGZ, ROWS, QW), BF),
            pltpu.VMEM((KPOS, HEAD), BF),
            pltpu.VMEM((SHARD, HEAD), BF),
            pltpu.VMEM((BLK, VPOS), BF),
            pltpu.VMEM((128, HEAD), BF),
            pltpu.VMEM((2, 2, ROWS, QH), BF),
            pltpu.VMEM((4, HEADS * HEAD, COLS), BF),
            pltpu.VMEM((KPOS, 2 * QH), F32),
            pltpu.VMEM((KPOS, 2 * QH), F32),
            pltpu.VMEM((VPOS, 2 * QH), BF),
            pltpu.VMEM((8, 2 * QH), F32),
            pltpu.VMEM((8, 2 * QH), F32),
            pltpu.VMEM((2 * RINGZ, BLK, QH), BF),
            pltpu.VMEM((RINGZ, BLK, QH), BF),
            pltpu.VMEM((RINGZ, BLK, QH), BF),
            pltpu.VMEM((RINGZ, BLK, QH), BF),
            pltpu.VMEM((RINGZ, BLK, QH), BF),
            pltpu.VMEM((ROWS, HEADS * HEAD), BF),
            pltpu.VMEM((RINGZ, ROWS, HEADS * HEAD), BF),
            pltpu.VMEM((4, RINGZ, ROWS, COLS), BF),
            dma((9,)), dma((6,)), dma((6,)), dma((9,)), dma((9,)),
            dma((RINGZ,)), dma((2 * RINGZ,)), dma((RINGZ,)),
            dma((RINGZ,)), dma((RINGZ,)), dma((RINGZ,)), dma((RINGZ,)), dma((RINGZ,)),
            dma((RINGZ,)), dma((RINGZ,)), dma((4 * RINGZ,)), dma((4 * RINGZ,)),
        ],
        compiler_params=pltpu.CompilerParams(
            collective_id=0, has_side_effects=True, vmem_limit_bytes=62 * 2**20
        ),
        cost_estimate=pl.CostEstimate(
            flops=9 * 10**9, bytes_accessed=2 * 2**20, transcendentals=2048 * 4224
        ),
    )(q, k, v, ck, cv, length, branch, depth, w)
    terms = terms.reshape(RINGZ, 4 * ROWS, COLS).astype(F32)
    return jnp.sum(terms, axis=0).astype(BF)


def solution(mesh):
    in_specs = (
        P("ctx", "kvh"),
        P("ctx", "kvh"),
        P("ctx", "kvh"),
        P("ctx", "kvh"),
        P("ctx", "kvh"),
        P("ctx"),
        P("ctx"),
        P("ctx"),
        P("kvh", "ctx"),
    )
    return jax.shard_map(
        local, mesh=mesh, in_specs=in_specs, out_specs=P("kvh", "ctx"), check_vma=False
    )
```

```python
import math

import jax
import jax.numpy as jnp
from jax import lax
from jax.experimental import pallas as pl
from jax.experimental.pallas import tpu as pltpu
from jax.sharding import PartitionSpec as P

MESH = pl.DeviceIdType.MESH
BF = jnp.bfloat16
F32 = jnp.float32
HEAD = 128
HEADS = 8
ROWS = 16
RINGZ = 8
SHARD = 2048
PAIR = 2 * SHARD
CAND = 2 * ROWS
KPOS = PAIR + CAND
VPOS = PAIR + 128
QH = HEADS * ROWS
QW = HEADS * HEAD + 128
BLK = HEAD + 16
COLS = 256
NEG = -1e30
SCALE = math.log2(math.e) / math.sqrt(HEAD)
CQ = 256
CP = 1024
WROWS = HEADS * HEAD // RINGZ
FAR_FIRST = (4, 3, 5, 2, 6, 1, 7)
QUERY_ORDER = ((1, 0), (7, 0), (0, 1), (2, 0), (6, 0), (4, 0), (3, 0), (5, 0))
JOINED = ()
JOIN_EARLY = 0
STEPS = ((0, 2), (14, 4), (1, 12), (6, 10), (3, 15), (5, 13), (9, 7), (11, 8))
ARRIVE = ((2, 14), (4, 12), (1, 8), (6, 10), (3, 15), (5, 13), (9, 7), (11,))
W_AT = (0, 0, 0, 1, 2, 3, 4, 5, 8)


def split2(x):
    hi = x.astype(BF)
    lo = (x - hi.astype(F32)).astype(BF)
    return hi, lo


def kernel(
    q_hbm, k_hbm, v_hbm, ck_hbm, cv_hbm, len_hbm, branch_hbm, depth_hbm, w_hbm,
    terms,
    ints, qall, kbuf, vraw, vt, cvraw, cinfo, wbuf, sa, sb, pbuf, ma, mb, part, yget, zsend, got, gotd, blk, attn, prod,
    loc, kv_s, kv_r, w_s, w_r, q_s, q_r, r_s, y_s, y_r, p_s, p_r, d_r, a_s, a_r, t_s, t_r,
):
    ctx = lax.axis_index("ctx")
    kvh = lax.axis_index("kvh")
    z = ctx // 4
    yh = (ctx // 2) % 2
    core = ctx % 2
    quarter = ctx % 4
    partner = (quarter + 2) % 4

    def plane(dz, so):
        zz = (z + dz) % RINGZ
        yy = (yh + so) % 2
        return (zz * 4 + yy * 2 + core, kvh)

    sibling = (ctx + 1 - 2 * core, kvh)

    def group(j, k):
        return (ctx - quarter + j, k)

    bar = pltpu.get_barrier_semaphore()
    peers = [plane(dz, so) for dz in range(1, RINGZ) for so in range(2)]
    peers += [group((quarter + j) % 4, kvh) for j in range(1, 4)]
    peers += [group(j, (kvh + dk) % RINGZ) for dk in range(1, RINGZ) for j in range(4)]
    for peer in peers:
        pl.semaphore_signal(bar, inc=1, device_id=peer, device_id_type=MESH)

    mine = pl.multiple_of(core * SHARD, SHARD)
    cmine = pl.multiple_of(PAIR + core * ROWS, ROWS)
    crow = pl.multiple_of(core * ROWS, ROWS)
    loads = [
        pltpu.make_async_copy(q_hbm, qall.at[0, :, pl.ds(0, HEADS * HEAD)], loc.at[0]),
        pltpu.make_async_copy(len_hbm, ints.at[0], loc.at[6]),
        pltpu.make_async_copy(branch_hbm, ints.at[1], loc.at[7]),
        pltpu.make_async_copy(depth_hbm, ints.at[2], loc.at[8]),
        pltpu.make_async_copy(k_hbm, kbuf.at[pl.ds(mine, SHARD)], loc.at[1]),
        pltpu.make_async_copy(ck_hbm, kbuf.at[pl.ds(cmine, ROWS)], loc.at[3]),
        pltpu.make_async_copy(cv_hbm, cvraw.at[pl.ds(crow, ROWS)], loc.at[4]),
        pltpu.make_async_copy(v_hbm, vraw, loc.at[2]),
        pltpu.make_async_copy(w_hbm, wbuf.at[quarter], loc.at[5]),
    ]
    for copy in loads:
        copy.start()
    for copy in loads[:4]:
        copy.wait()

    lane = lax.broadcasted_iota(jnp.int32, (ROWS, QH), 1)
    sub = lax.broadcasted_iota(jnp.int32, (ROWS, QH), 0)
    lane_row = lane % ROWS
    meta = jnp.zeros((ROWS, QH), jnp.int32)
    cb = jnp.zeros((ROWS, QH), jnp.int32)
    cd = jnp.zeros((ROWS, QH), jnp.int32)
    for i in range(ROWS):
        n = ints[0, i]
        b = ints[1, i]
        d = ints[2, i]
        high = n // 256
        col = jnp.where(
            sub == 0, high, jnp.where(sub == 1, n - high * 256, jnp.where(sub == 2, b, d))
        )
        meta = jnp.where(lane_row == i, col, meta)
        cb = jnp.where(sub == i, b, cb)
        cd = jnp.where(sub == i, d, cd)
    qall[0, :, HEADS * HEAD :] = meta.astype(F32).astype(BF)
    cinfo[core, 0] = cb.astype(F32).astype(BF)
    cinfo[core, 1] = cd.astype(F32).astype(BF)
    pbuf[KPOS:, :] = jnp.zeros((VPOS - KPOS, 2 * QH), BF)
    vt[HEAD:, :] = jnp.ones((BLK - HEAD, VPOS), BF)
    cvraw[CAND:, :] = jnp.zeros((128 - CAND, HEAD), BF)

    def block_to(src, dst, send, recv, peer):
        return pltpu.make_async_remote_copy(
            src_ref=src, dst_ref=dst, send_sem=send, recv_sem=recv, device_id=peer, device_id_type=MESH
        )

    def arrived(dst, recv):
        block_to(dst, dst, recv, recv, sibling).wait_recv()

    across = plane(0, 1)

    def query_z(dz):
        back = (RINGZ - dz) % RINGZ
        return block_to(
            qall.at[0], qall.at[2 * back], q_s.at[dz], q_r.at[2 * back], plane(dz, 0)
        )

    def query_d(dz):
        back = (RINGZ - dz) % RINGZ
        return block_to(
            qall.at[0], qall.at[2 * back + 1], r_s.at[dz], q_r.at[2 * back + 1], plane(dz, 1)
        )

    def query_y(dz):
        return block_to(
            qall.at[2 * dz], qall.at[2 * dz + 1], r_s.at[dz], q_r.at[2 * dz + 1], across
        )

    def part_y(dz):
        return block_to(part.at[2 * dz + 1], yget.at[dz], y_s.at[dz], y_r.at[dz], across)

    def part_z(dz):
        back = (RINGZ - dz) % RINGZ
        src = zsend.at[dz] if dz in JOINED else part.at[2 * dz]
        return block_to(src, got.at[back], p_s.at[dz], p_r.at[back], plane(dz, 0))

    def part_d(dz):
        back = (RINGZ - dz) % RINGZ
        return block_to(
            part.at[2 * dz + 1], gotd.at[back], y_s.at[dz], d_r.at[back], plane(dz, 1)
        )

    def w_across(n, slab):
        rows = pl.ds(n * WROWS, WROWS)
        return block_to(
            wbuf.at[slab, rows], wbuf.at[slab, rows], w_s.at[n], w_r.at[n], across
        )

    def w_relay(slab):
        return block_to(wbuf.at[slab], wbuf.at[slab], w_s.at[RINGZ], w_r.at[RINGZ], sibling)

    def swap(n, ref):
        return block_to(ref, ref, kv_s.at[n], kv_r.at[n], sibling)

    def swaps(side):
        base = pl.multiple_of(side * SHARD, SHARD)
        cbase = pl.multiple_of(PAIR + side * ROWS, ROWS)
        rbase = pl.multiple_of(side * ROWS, ROWS)
        return [
            swap(0, kbuf.at[pl.ds(base, SHARD)]),
            swap(1, kbuf.at[pl.ds(cbase, ROWS)]),
            swap(2, cvraw.at[pl.ds(rbase, ROWS)]),
            swap(3, cinfo.at[side]),
            swap(4, vt.at[pl.ds(0, HEAD), pl.ds(base, SHARD)]),
            swap(5, wbuf.at[quarter - core + side]),
        ]

    pl.semaphore_wait(bar, len(peers))
    for dz, so in QUERY_ORDER:
        (query_d(dz) if dz and so else query_y(0) if so else query_z(dz)).start()
    out_swaps = swaps(core)
    in_swaps = swaps(1 - core)
    for copy in loads[4:7]:
        copy.wait()
    for copy in out_swaps[:4]:
        copy.start()
    loads[7].wait()
    for j in range(0, SHARD, 128):
        vt[0:HEAD, pl.ds(pl.multiple_of(mine + j, 128), 128)] = vraw[j : j + 128, :].T
    out_swaps[4].start()
    loads[8].wait()
    out_swaps[5].start()
    base = (ctx - core) * SHARD
    pos_sub = lax.broadcasted_iota(jnp.int32, (CQ, QH), 0)

    def read_stats(st):
        return st[0:1] + st[1:2] + st[2:3], st[3:4] + st[4:5]

    def write_stats(m, total):
        m_hi = m.astype(BF)
        m_mid, m_lo = split2(m - m_hi.astype(F32))
        l_hi, l_lo = split2(total)
        row = lax.broadcasted_iota(jnp.int32, (BLK - HEAD, m.shape[1]), 0)
        stats = jnp.zeros((BLK - HEAD, m.shape[1]), F32)
        for n, x in enumerate((m_hi, m_mid, m_lo, l_hi, l_lo)):
            stats = jnp.where(row == n, x.astype(F32), stats)
        return stats.astype(BF)

    def load_q(pair):
        parts = []
        infos = []
        for slot in pair:
            for h in range(HEADS):
                parts.append(qall[slot, :, h * HEAD : (h + 1) * HEAD])
            infos.append(qall[slot, :, HEADS * HEAD :].astype(F32))
        q = jnp.concatenate(parts, axis=0).astype(F32) * SCALE
        hi, lo = split2(q)
        lens = [(f[0:1] * 256.0 + f[1:2]).astype(jnp.int32) - base for f in infos]
        return jnp.concatenate([hi, lo], axis=1), lens, infos

    def score(q, pos, width):
        k = kbuf[pos : pos + width, :]
        return lax.dot_general(
            jnp.concatenate([k, k], axis=1), q, (((1,), (1,)), ((), ())),
            preferred_element_type=F32,
        )

    def fused(new, old, parity):
        s_new, s_old = (sa, sb) if parity == 0 else (sb, sa)
        m_new, m_old = (ma, mb) if parity == 0 else (mb, ma)
        if new is not None:
            q, lens, infos = load_q(new)
            top = jnp.full((8, 2 * QH), NEG, F32)
            s = score(q, PAIR, CAND)
            cbr = jnp.concatenate([cinfo[0, 0], cinfo[1, 0]], axis=0).astype(F32)
            cde = jnp.concatenate([cinfo[0, 1], cinfo[1, 1]], axis=0).astype(F32)
            s = jnp.concatenate(
                [
                    jnp.where(
                        (cbr == f[2:3]) & (cde <= f[3:4]), s[:, n * QH : (n + 1) * QH], NEG
                    )
                    for n, f in enumerate(infos)
                ],
                axis=1,
            )
            s_new[PAIR:KPOS, :] = s
            for j in range(0, CAND, 8):
                top = jnp.maximum(top, s[j : j + 8, :])
        if old is not None:
            m = m_old[0:1, :]
            acc = None
            start = 0
        for pos in range(0, PAIR, CQ):
            if new is not None:
                s = score(q, pos, CQ)
                s = jnp.concatenate(
                    [
                        jnp.where(pos_sub < n - pos, s[:, j * QH : (j + 1) * QH], NEG)
                        for j, n in enumerate(lens)
                    ],
                    axis=1,
                )
                s_new[pos : pos + CQ, :] = s
                for j in range(0, CQ, 8):
                    top = jnp.maximum(top, s[j : j + 8, :])
            if old is not None:
                pbuf[pos : pos + CQ, :] = jnp.exp2(s_old[pos : pos + CQ, :] - m).astype(BF)
                end = pos + CQ
                if end == PAIR:
                    pbuf[PAIR:KPOS, :] = jnp.exp2(s_old[PAIR:KPOS, :] - m).astype(BF)
                    end = VPOS
                if end - start >= CP:
                    term = jnp.dot(
                        vt[:, start:end], pbuf[start:end, :], preferred_element_type=F32
                    )
                    acc = term if acc is None else acc + term
                    start = end
        if old is not None:
            total = acc[HEAD : HEAD + 1]
            stats = write_stats(m, total)
            for n, slot in enumerate(old):
                lanes = slice(n * QH, (n + 1) * QH)
                part[slot, 0:HEAD, :] = acc[0:HEAD, lanes].astype(BF)
                part[slot, HEAD:, :] = stats[:, lanes]
        if new is not None:
            m_new[...] = jnp.broadcast_to(jnp.max(top, axis=0, keepdims=True), (8, 2 * QH))

    def nth(t):
        pair = []
        for side in range(2):
            slot = jnp.int32(STEPS[0][side])
            for n in range(1, RINGZ):
                slot = jnp.where(t == n, STEPS[n][side], slot)
            pair.append(slot)
        return pair

    def ready(t):
        for slot in ARRIVE[t]:
            arrived(qall.at[slot], q_r.at[slot])
            if slot % 2 == 0 and (slot // 2, 1) not in QUERY_ORDER:
                query_y(slot // 2).start()

    def finished(t):
        for slot in STEPS[t]:
            dz = slot // 2
            if slot % 2:
                (part_y if dz in JOINED or dz == 0 else part_d)(dz).start()
            elif dz and dz not in JOINED:
                part_z(dz).start()
        for n in range(W_AT[t], W_AT[t + 1]):
            w_across(n, quarter).start()

    def at(i, fn, steps):
        for n, t in enumerate(steps):
            pl.when(i == n)(lambda t=t: fn(t))

    for n in range(4):
        in_swaps[n].wait_recv()
    ready(0)
    fused(STEPS[0], None, 0)
    in_swaps[4].wait_recv()
    vt[0:HEAD, PAIR:] = cvraw[...].T

    def body(i, carry):
        a, b, c = nth(2 * i), nth(2 * i + 1), nth(2 * i + 2)
        at(i, ready, (1, 3, 5))
        fused(b, a, 1)
        at(i, finished, (0, 2, 4))
        at(i, ready, (2, 4, 6))
        fused(c, b, 0)
        at(i, finished, (1, 3, 5))
        return carry

    lax.fori_loop(0, 3, body, 0)
    ready(7)
    fused(STEPS[7], STEPS[6], 1)
    finished(6)
    def merge(stats, accs):
        top = stats[0][0]
        for m, _ in stats[1:]:
            top = jnp.maximum(top, m)
        acc = total = None
        for (m, l), x in zip(stats, accs):
            f = jnp.exp2(m - top)
            total = l * f if total is None else total + l * f
            term = x.astype(F32) * f
            acc = term if acc is None else acc + term
        return acc, top, total

    def join(dz, dst):
        arrived(yget.at[dz], y_r.at[dz])
        refs = (part.at[2 * dz], yget.at[dz])
        acc, top, total = merge(
            [read_stats(ref[HEAD:, :].astype(F32)) for ref in refs], [ref[0:HEAD, :] for ref in refs]
        )
        dst[0:HEAD, :] = acc.astype(BF)
        dst[HEAD:, :] = write_stats(top, total)

    for dz in JOINED[:JOIN_EARLY]:
        join(dz, zsend.at[dz])
        part_z(dz).start()
    fused(None, STEPS[7], 0)
    finished(7)
    for dz in JOINED[JOIN_EARLY:]:
        join(dz, zsend.at[dz])
        part_z(dz).start()
    join(0, got.at[0])

    for dz in range(1, RINGZ):
        arrived(got.at[dz], p_r.at[dz])
    singles = [dz for dz in range(1, RINGZ) if dz not in JOINED]
    for dz in singles:
        back = RINGZ - dz
        arrived(gotd.at[back], d_r.at[back])
    refs = [got.at[dz] for dz in range(RINGZ)] + [gotd.at[(RINGZ - dz) % RINGZ] for dz in singles]
    acc, top, total = merge(
        [read_stats(ref[HEAD:, :].astype(F32)) for ref in refs], [ref[0:HEAD, :] for ref in refs]
    )
    own = (acc / total).T.astype(BF)
    for h in range(HEADS):
        blk[:, h * HEAD : (h + 1) * HEAD] = own[h * ROWS : (h + 1) * ROWS, :]

    def attn_out(dz):
        back = (RINGZ - dz) % RINGZ
        return block_to(blk, attn.at[back], a_s.at[dz], a_r.at[back], plane(dz, 0))

    for dz in FAR_FIRST:
        attn_out(dz).start()
    attn[0] = blk[...]
    for n in range(RINGZ):
        w_across(n, partner).wait_recv()
    w_relay(partner).start()

    in_swaps[5].wait_recv()
    w_relay((partner + 1 - 2 * core)).wait_recv()
    me = kvh * 4 + quarter

    def term_copy(i, n):
        return block_to(
            prod.at[i, n], terms.at[me], t_s.at[i * RINGZ + n], t_r.at[me],
            group((quarter + i) % 4, (z + n) % RINGZ),
        )

    def own_term(n):
        return pltpu.make_async_copy(prod.at[0, n], terms.at[me], t_s.at[n])

    for dz in range(1, RINGZ):
        arrived(attn.at[dz], a_r.at[dz])
    rows = jnp.concatenate([attn[n] for n in range(RINGZ)], axis=0)
    for i in (2, 3, 1, 0):
        j = (quarter + i) % 4
        res = jnp.dot(rows, wbuf[j], preferred_element_type=F32).astype(BF)
        for n in range(RINGZ):
            prod[i, n] = res[n * ROWS : (n + 1) * ROWS, :]
        for n in range(RINGZ):
            if i:
                term_copy(i, n).start()
            else:
                here = (z + n) % RINGZ == kvh

                @pl.when(here)
                def _():
                    own_term(n).start()

                @pl.when(jnp.logical_not(here))
                def _():
                    term_copy(i, n).start()

    for copy in out_swaps + [w_relay(partner)]:
        copy.wait_send()
    for dz in range(RINGZ):
        (query_d if dz and (dz, 1) in QUERY_ORDER else query_y)(dz).wait_send()
        (part_y if dz in JOINED or dz == 0 else part_d)(dz).wait_send()
        w_across(dz, quarter).wait_send()
        if dz:
            query_z(dz).wait_send()
            part_z(dz).wait_send()
            attn_out(dz).wait_send()
    for i in range(4):
        for n in range(RINGZ):
            if i:
                term_copy(i, n).wait_send()
            else:
                here = (z + n) % RINGZ == kvh

                @pl.when(here)
                def _():
                    own_term(n).wait()

                @pl.when(jnp.logical_not(here))
                def _():
                    term_copy(i, n).wait_send()

    for idx in range(4 * RINGZ):

        @pl.when(idx != me)
        def _():
            arrived(terms.at[idx], t_r.at[idx])


def local(q, k, v, ck, cv, length, branch, depth, w):
    hbm = pl.BlockSpec(memory_space=pl.ANY)
    dma = pltpu.SemaphoreType.DMA
    terms = pl.pallas_call(
        kernel,
        out_shape=jax.ShapeDtypeStruct((4 * RINGZ, ROWS, COLS), BF),
        in_specs=[hbm] * 9,
        out_specs=hbm,
        scratch_shapes=[
            pltpu.SMEM((3, ROWS), jnp.int32),
            pltpu.VMEM((2 * RINGZ, ROWS, QW), BF),
            pltpu.VMEM((KPOS, HEAD), BF),
            pltpu.VMEM((SHARD, HEAD), BF),
            pltpu.VMEM((BLK, VPOS), BF),
            pltpu.VMEM((128, HEAD), BF),
            pltpu.VMEM((2, 2, ROWS, QH), BF),
            pltpu.VMEM((4, HEADS * HEAD, COLS), BF),
            pltpu.VMEM((KPOS, 2 * QH), F32),
            pltpu.VMEM((KPOS, 2 * QH), F32),
            pltpu.VMEM((VPOS, 2 * QH), BF),
            pltpu.VMEM((8, 2 * QH), F32),
            pltpu.VMEM((8, 2 * QH), F32),
            pltpu.VMEM((2 * RINGZ, BLK, QH), BF),
            pltpu.VMEM((RINGZ, BLK, QH), BF),
            pltpu.VMEM((RINGZ, BLK, QH), BF),
            pltpu.VMEM((RINGZ, BLK, QH), BF),
            pltpu.VMEM((RINGZ, BLK, QH), BF),
            pltpu.VMEM((ROWS, HEADS * HEAD), BF),
            pltpu.VMEM((RINGZ, ROWS, HEADS * HEAD), BF),
            pltpu.VMEM((4, RINGZ, ROWS, COLS), BF),
            dma((9,)), dma((6,)), dma((6,)), dma((9,)), dma((9,)),
            dma((RINGZ,)), dma((2 * RINGZ,)), dma((RINGZ,)),
            dma((RINGZ,)), dma((RINGZ,)), dma((RINGZ,)), dma((RINGZ,)), dma((RINGZ,)),
            dma((RINGZ,)), dma((RINGZ,)), dma((4 * RINGZ,)), dma((4 * RINGZ,)),
        ],
        compiler_params=pltpu.CompilerParams(
            collective_id=0, has_side_effects=True, vmem_limit_bytes=62 * 2**20
        ),
        cost_estimate=pl.CostEstimate(
            flops=9 * 10**9, bytes_accessed=2 * 2**20, transcendentals=2048 * 4224
        ),
    )(q, k, v, ck, cv, length, branch, depth, w)
    terms = terms.reshape(RINGZ, 4 * ROWS, COLS).astype(F32)
    return jnp.sum(terms, axis=0).astype(BF)


def solution(mesh):
    in_specs = (
        P("ctx", "kvh"),
        P("ctx", "kvh"),
        P("ctx", "kvh"),
        P("ctx", "kvh"),
        P("ctx", "kvh"),
        P("ctx"),
        P("ctx"),
        P("ctx"),
        P("kvh", "ctx"),
    )
    return jax.shard_map(
        local, mesh=mesh, in_specs=in_specs, out_specs=P("kvh", "ctx"), check_vma=False
    )
```

```python
import math

import jax
import jax.numpy as jnp
from jax import lax
from jax.experimental import pallas as pl
from jax.experimental.pallas import tpu as pltpu
from jax.sharding import PartitionSpec as P

MESH = pl.DeviceIdType.MESH
BF = jnp.bfloat16
F32 = jnp.float32
HEAD = 128
HEADS = 8
ROWS = 16
RINGZ = 8
SHARD = 2048
PAIR = 2 * SHARD
CAND = 2 * ROWS
KPOS = PAIR + CAND
VPOS = PAIR + 128
QH = HEADS * ROWS
QW = HEADS * HEAD + 128
BLK = HEAD + 16
COLS = 256
NEG = -1e30
SCALE = math.log2(math.e) / math.sqrt(HEAD)
CQ = 256
CP = 1024
WROWS = HEADS * HEAD // RINGZ
FAR_FIRST = (4, 3, 5, 2, 6, 1, 7)
QUERY_ORDER = ((1, 0), (7, 0), (0, 1), (2, 0), (6, 0), (4, 0), (3, 0), (5, 0))
JOINED = ()
JOIN_EARLY = 0
STEPS = ((0, 2), (14, 4), (1, 12), (6, 10), (3, 15), (5, 13), (9, 7), (11, 8))
ARRIVE = ((2, 14), (4, 12), (1, 8), (6, 10), (3, 15), (5, 13), (9, 7), (11,))
W_AT = (0, 0, 0, 1, 2, 3, 4, 5, 8)


def split2(x):
    hi = x.astype(BF)
    lo = (x - hi.astype(F32)).astype(BF)
    return hi, lo


def kernel(
    q_hbm, k_hbm, v_hbm, ck_hbm, cv_hbm, len_hbm, branch_hbm, depth_hbm, w_hbm,
    terms,
    ints, qall, kbuf, vraw, vt, cvraw, cinfo, wbuf, sa, sb, pbuf, ma, mb, part, yget, zsend, got, gotd, blk, attn, prod,
    loc, kv_s, kv_r, w_s, w_r, q_s, q_r, r_s, y_s, y_r, p_s, p_r, d_r, a_s, a_r, t_s, t_r,
):
    ctx = lax.axis_index("ctx")
    kvh = lax.axis_index("kvh")
    z = ctx // 4
    yh = (ctx // 2) % 2
    core = ctx % 2
    quarter = ctx % 4
    partner = (quarter + 2) % 4

    def plane(dz, so):
        zz = (z + dz) % RINGZ
        yy = (yh + so) % 2
        return (zz * 4 + yy * 2 + core, kvh)

    sibling = (ctx + 1 - 2 * core, kvh)

    def group(j, k):
        return (ctx - quarter + j, k)

    bar = pltpu.get_barrier_semaphore()
    peers = [plane(dz, so) for dz in range(1, RINGZ) for so in range(2)]
    peers += [group((quarter + j) % 4, kvh) for j in range(1, 4)]
    peers += [group(j, (kvh + dk) % RINGZ) for dk in range(1, RINGZ) for j in range(4)]
    for peer in peers:
        pl.semaphore_signal(bar, inc=1, device_id=peer, device_id_type=MESH)

    mine = pl.multiple_of(core * SHARD, SHARD)
    cmine = pl.multiple_of(PAIR + core * ROWS, ROWS)
    crow = pl.multiple_of(core * ROWS, ROWS)
    loads = [
        pltpu.make_async_copy(q_hbm, qall.at[0, :, pl.ds(0, HEADS * HEAD)], loc.at[0]),
        pltpu.make_async_copy(len_hbm, ints.at[0], loc.at[6]),
        pltpu.make_async_copy(branch_hbm, ints.at[1], loc.at[7]),
        pltpu.make_async_copy(depth_hbm, ints.at[2], loc.at[8]),
        pltpu.make_async_copy(k_hbm, kbuf.at[pl.ds(mine, SHARD)], loc.at[1]),
        pltpu.make_async_copy(ck_hbm, kbuf.at[pl.ds(cmine, ROWS)], loc.at[3]),
        pltpu.make_async_copy(cv_hbm, cvraw.at[pl.ds(crow, ROWS)], loc.at[4]),
        pltpu.make_async_copy(v_hbm, vraw, loc.at[2]),
        pltpu.make_async_copy(w_hbm, wbuf.at[quarter], loc.at[5]),
    ]
    for copy in loads:
        copy.start()
    for copy in loads[:4]:
        copy.wait()

    lane = lax.broadcasted_iota(jnp.int32, (ROWS, QH), 1)
    sub = lax.broadcasted_iota(jnp.int32, (ROWS, QH), 0)
    lane_row = lane % ROWS
    meta = jnp.zeros((ROWS, QH), jnp.int32)
    cb = jnp.zeros((ROWS, QH), jnp.int32)
    cd = jnp.zeros((ROWS, QH), jnp.int32)
    for i in range(ROWS):
        n = ints[0, i]
        b = ints[1, i]
        d = ints[2, i]
        high = n // 256
        col = jnp.where(
            sub == 0, high, jnp.where(sub == 1, n - high * 256, jnp.where(sub == 2, b, d))
        )
        meta = jnp.where(lane_row == i, col, meta)
        cb = jnp.where(sub == i, b, cb)
        cd = jnp.where(sub == i, d, cd)
    qall[0, :, HEADS * HEAD :] = meta.astype(F32).astype(BF)
    cinfo[core, 0] = cb.astype(F32).astype(BF)
    cinfo[core, 1] = cd.astype(F32).astype(BF)
    pbuf[KPOS:, :] = jnp.zeros((VPOS - KPOS, 2 * QH), BF)
    vt[HEAD:, :] = jnp.ones((BLK - HEAD, VPOS), BF)
    cvraw[CAND:, :] = jnp.zeros((128 - CAND, HEAD), BF)

    def block_to(src, dst, send, recv, peer):
        return pltpu.make_async_remote_copy(
            src_ref=src, dst_ref=dst, send_sem=send, recv_sem=recv, device_id=peer, device_id_type=MESH
        )

    def arrived(dst, recv):
        block_to(dst, dst, recv, recv, sibling).wait_recv()

    across = plane(0, 1)

    def query_z(dz):
        back = (RINGZ - dz) % RINGZ
        return block_to(
            qall.at[0], qall.at[2 * back], q_s.at[dz], q_r.at[2 * back], plane(dz, 0)
        )

    def query_d(dz):
        back = (RINGZ - dz) % RINGZ
        return block_to(
            qall.at[0], qall.at[2 * back + 1], r_s.at[dz], q_r.at[2 * back + 1], plane(dz, 1)
        )

    def query_y(dz):
        return block_to(
            qall.at[2 * dz], qall.at[2 * dz + 1], r_s.at[dz], q_r.at[2 * dz + 1], across
        )

    def part_y(dz):
        return block_to(part.at[2 * dz + 1], yget.at[dz], y_s.at[dz], y_r.at[dz], across)

    def part_z(dz):
        back = (RINGZ - dz) % RINGZ
        src = zsend.at[dz] if dz in JOINED else part.at[2 * dz]
        return block_to(src, got.at[back], p_s.at[dz], p_r.at[back], plane(dz, 0))

    def part_d(dz):
        back = (RINGZ - dz) % RINGZ
        return block_to(
            part.at[2 * dz + 1], gotd.at[back], y_s.at[dz], d_r.at[back], plane(dz, 1)
        )

    def w_across(n, slab):
        rows = pl.ds(n * WROWS, WROWS)
        return block_to(
            wbuf.at[slab, rows], wbuf.at[slab, rows], w_s.at[n], w_r.at[n], across
        )

    def w_relay(slab):
        return block_to(wbuf.at[slab], wbuf.at[slab], w_s.at[RINGZ], w_r.at[RINGZ], sibling)

    def swap(n, ref):
        return block_to(ref, ref, kv_s.at[n], kv_r.at[n], sibling)

    def swaps(side):
        base = pl.multiple_of(side * SHARD, SHARD)
        cbase = pl.multiple_of(PAIR + side * ROWS, ROWS)
        rbase = pl.multiple_of(side * ROWS, ROWS)
        return [
            swap(0, kbuf.at[pl.ds(base, SHARD)]),
            swap(1, kbuf.at[pl.ds(cbase, ROWS)]),
            swap(2, cvraw.at[pl.ds(rbase, ROWS)]),
            swap(3, cinfo.at[side]),
            swap(4, vt.at[pl.ds(0, HEAD), pl.ds(base, SHARD)]),
            swap(5, wbuf.at[quarter - core + side]),
        ]

    pl.semaphore_wait(bar, len(peers))
    for dz, so in QUERY_ORDER:
        (query_d(dz) if dz and so else query_y(0) if so else query_z(dz)).start()
    out_swaps = swaps(core)
    in_swaps = swaps(1 - core)
    for copy in loads[4:7]:
        copy.wait()
    for copy in out_swaps[:4]:
        copy.start()
    loads[7].wait()
    for j in range(0, SHARD, 128):
        vt[0:HEAD, pl.ds(pl.multiple_of(mine + j, 128), 128)] = vraw[j : j + 128, :].T
    out_swaps[4].start()
    loads[8].wait()
    out_swaps[5].start()
    base = (ctx - core) * SHARD
    pos_sub = lax.broadcasted_iota(jnp.int32, (CQ, QH), 0)

    def read_stats(st):
        return st[0:1] + st[1:2] + st[2:3], st[3:4] + st[4:5]

    def write_stats(m, total):
        m_hi = m.astype(BF)
        m_mid, m_lo = split2(m - m_hi.astype(F32))
        l_hi, l_lo = split2(total)
        row = lax.broadcasted_iota(jnp.int32, (BLK - HEAD, m.shape[1]), 0)
        stats = jnp.zeros((BLK - HEAD, m.shape[1]), F32)
        for n, x in enumerate((m_hi, m_mid, m_lo, l_hi, l_lo)):
            stats = jnp.where(row == n, x.astype(F32), stats)
        return stats.astype(BF)

    def load_q(pair):
        parts = []
        infos = []
        for slot in pair:
            for h in range(HEADS):
                parts.append(qall[slot, :, h * HEAD : (h + 1) * HEAD])
            infos.append(qall[slot, :, HEADS * HEAD :].astype(F32))
        q = jnp.concatenate(parts, axis=0).astype(F32) * SCALE
        hi, lo = split2(q)
        lens = [(f[0:1] * 256.0 + f[1:2]).astype(jnp.int32) - base for f in infos]
        return jnp.concatenate([hi, lo], axis=1), lens, infos

    def score(q, pos, width):
        k = kbuf[pos : pos + width, :]
        return lax.dot_general(
            jnp.concatenate([k, k], axis=1), q, (((1,), (1,)), ((), ())),
            preferred_element_type=F32,
        )

    def fused(new, old, parity):
        s_new, s_old = (sa, sb) if parity == 0 else (sb, sa)
        m_new, m_old = (ma, mb) if parity == 0 else (mb, ma)
        if new is not None:
            q, lens, infos = load_q(new)
            top = jnp.full((8, 2 * QH), NEG, F32)
            s = score(q, PAIR, CAND)
            cbr = jnp.concatenate([cinfo[0, 0], cinfo[1, 0]], axis=0).astype(F32)
            cde = jnp.concatenate([cinfo[0, 1], cinfo[1, 1]], axis=0).astype(F32)
            s = jnp.concatenate(
                [
                    jnp.where(
                        (cbr == f[2:3]) & (cde <= f[3:4]), s[:, n * QH : (n + 1) * QH], NEG
                    )
                    for n, f in enumerate(infos)
                ],
                axis=1,
            )
            s_new[PAIR:KPOS, :] = s
            for j in range(0, CAND, 8):
                top = jnp.maximum(top, s[j : j + 8, :])
        if old is not None:
            m = m_old[0:1, :]
            acc = None
            start = 0
        for pos in range(0, PAIR, CQ):
            if new is not None:
                s = score(q, pos, CQ)
                s = jnp.concatenate(
                    [
                        jnp.where(pos_sub < n - pos, s[:, j * QH : (j + 1) * QH], NEG)
                        for j, n in enumerate(lens)
                    ],
                    axis=1,
                )
                s_new[pos : pos + CQ, :] = s
                for j in range(0, CQ, 8):
                    top = jnp.maximum(top, s[j : j + 8, :])
            if old is not None:
                pbuf[pos : pos + CQ, :] = jnp.exp2(s_old[pos : pos + CQ, :] - m).astype(BF)
                end = pos + CQ
                if end == PAIR:
                    pbuf[PAIR:KPOS, :] = jnp.exp2(s_old[PAIR:KPOS, :] - m).astype(BF)
                    end = VPOS
                if end - start >= CP:
                    term = jnp.dot(
                        vt[:, start:end], pbuf[start:end, :], preferred_element_type=F32
                    )
                    acc = term if acc is None else acc + term
                    start = end
        if old is not None:
            total = acc[HEAD : HEAD + 1]
            stats = write_stats(m, total)
            for n, slot in enumerate(old):
                lanes = slice(n * QH, (n + 1) * QH)
                part[slot, 0:HEAD, :] = acc[0:HEAD, lanes].astype(BF)
                part[slot, HEAD:, :] = stats[:, lanes]
        if new is not None:
            m_new[...] = jnp.broadcast_to(jnp.max(top, axis=0, keepdims=True), (8, 2 * QH))

    def nth(t):
        pair = []
        for side in range(2):
            slot = jnp.int32(STEPS[0][side])
            for n in range(1, RINGZ):
                slot = jnp.where(t == n, STEPS[n][side], slot)
            pair.append(slot)
        return pair

    def ready(t):
        for slot in ARRIVE[t]:
            arrived(qall.at[slot], q_r.at[slot])
            if slot % 2 == 0 and (slot // 2, 1) not in QUERY_ORDER:
                query_y(slot // 2).start()

    def finished(t):
        for slot in STEPS[t]:
            dz = slot // 2
            if slot % 2:
                (part_y if dz in JOINED or dz == 0 else part_d)(dz).start()
            elif dz and dz not in JOINED:
                part_z(dz).start()
        for n in range(W_AT[t], W_AT[t + 1]):
            w_across(n, quarter).start()

    def at(i, fn, steps):
        for n, t in enumerate(steps):
            pl.when(i == n)(lambda t=t: fn(t))

    for n in range(4):
        in_swaps[n].wait_recv()
    ready(0)
    fused(STEPS[0], None, 0)
    in_swaps[4].wait_recv()
    vt[0:HEAD, PAIR:] = cvraw[...].T

    def body(i, carry):
        a, b, c = nth(2 * i), nth(2 * i + 1), nth(2 * i + 2)
        at(i, ready, (1, 3, 5))
        fused(b, a, 1)
        at(i, finished, (0, 2, 4))
        at(i, ready, (2, 4, 6))
        fused(c, b, 0)
        at(i, finished, (1, 3, 5))
        return carry

    lax.fori_loop(0, 3, body, 0)
    ready(7)
    fused(STEPS[7], STEPS[6], 1)
    finished(6)
    def merge(stats, accs):
        top = stats[0][0]
        for m, _ in stats[1:]:
            top = jnp.maximum(top, m)
        acc = total = None
        for (m, l), x in zip(stats, accs):
            f = jnp.exp2(m - top)
            total = l * f if total is None else total + l * f
            term = x.astype(F32) * f
            acc = term if acc is None else acc + term
        return acc, top, total

    def join(dz, dst):
        arrived(yget.at[dz], y_r.at[dz])
        refs = (part.at[2 * dz], yget.at[dz])
        acc, top, total = merge(
            [read_stats(ref[HEAD:, :].astype(F32)) for ref in refs], [ref[0:HEAD, :] for ref in refs]
        )
        dst[0:HEAD, :] = acc.astype(BF)
        dst[HEAD:, :] = write_stats(top, total)

    for dz in JOINED[:JOIN_EARLY]:
        join(dz, zsend.at[dz])
        part_z(dz).start()
    fused(None, STEPS[7], 0)
    finished(7)
    for dz in JOINED[JOIN_EARLY:]:
        join(dz, zsend.at[dz])
        part_z(dz).start()
    join(0, got.at[0])

    for dz in range(1, RINGZ):
        arrived(got.at[dz], p_r.at[dz])
    singles = [dz for dz in range(1, RINGZ) if dz not in JOINED]
    for dz in singles:
        back = RINGZ - dz
        arrived(gotd.at[back], d_r.at[back])
    refs = [got.at[dz] for dz in range(RINGZ)] + [gotd.at[(RINGZ - dz) % RINGZ] for dz in singles]
    acc, top, total = merge(
        [read_stats(ref[HEAD:, :].astype(F32)) for ref in refs], [ref[0:HEAD, :] for ref in refs]
    )
    own = (acc / total).T.astype(BF)
    for h in range(HEADS):
        blk[:, h * HEAD : (h + 1) * HEAD] = own[h * ROWS : (h + 1) * ROWS, :]

    def attn_out(dz):
        back = (RINGZ - dz) % RINGZ
        return block_to(blk, attn.at[back], a_s.at[dz], a_r.at[back], plane(dz, 0))

    for dz in FAR_FIRST:
        attn_out(dz).start()
    attn[0] = blk[...]
    for n in range(RINGZ):
        w_across(n, partner).wait_recv()
    w_relay(partner).start()

    in_swaps[5].wait_recv()
    w_relay((partner + 1 - 2 * core)).wait_recv()
    me = kvh * 4 + quarter

    def term_copy(i, n):
        return block_to(
            prod.at[i, n], terms.at[me], t_s.at[i * RINGZ + n], t_r.at[me],
            group((quarter + i) % 4, (z + n) % RINGZ),
        )

    def own_term(n):
        return pltpu.make_async_copy(prod.at[0, n], terms.at[me], t_s.at[n])

    for some in ((0, 1, 7, 2, 6), (3, 5, 4)):
        for dz in some:
            if dz:
                arrived(attn.at[dz], a_r.at[dz])
        rows = jnp.concatenate([attn[n] for n in some], axis=0)
        for i in (2, 3, 1, 0):
            j = (quarter + i) % 4
            res = jnp.dot(rows, wbuf[j], preferred_element_type=F32).astype(BF)
            for m, n in enumerate(some):
                prod[i, n] = res[m * ROWS : (m + 1) * ROWS, :]
            for n in some:
                if i:
                    term_copy(i, n).start()
                else:
                    here = (z + n) % RINGZ == kvh

                    @pl.when(here)
                    def _():
                        own_term(n).start()

                    @pl.when(jnp.logical_not(here))
                    def _():
                        term_copy(i, n).start()

    for copy in out_swaps + [w_relay(partner)]:
        copy.wait_send()
    for dz in range(RINGZ):
        (query_d if dz and (dz, 1) in QUERY_ORDER else query_y)(dz).wait_send()
        (part_y if dz in JOINED or dz == 0 else part_d)(dz).wait_send()
        w_across(dz, quarter).wait_send()
        if dz:
            query_z(dz).wait_send()
            part_z(dz).wait_send()
            attn_out(dz).wait_send()
    for i in range(4):
        for n in range(RINGZ):
            if i:
                term_copy(i, n).wait_send()
            else:
                here = (z + n) % RINGZ == kvh

                @pl.when(here)
                def _():
                    own_term(n).wait()

                @pl.when(jnp.logical_not(here))
                def _():
                    term_copy(i, n).wait_send()

    for idx in range(4 * RINGZ):

        @pl.when(idx != me)
        def _():
            arrived(terms.at[idx], t_r.at[idx])


def local(q, k, v, ck, cv, length, branch, depth, w):
    hbm = pl.BlockSpec(memory_space=pl.ANY)
    dma = pltpu.SemaphoreType.DMA
    terms = pl.pallas_call(
        kernel,
        out_shape=jax.ShapeDtypeStruct((4 * RINGZ, ROWS, COLS), BF),
        in_specs=[hbm] * 9,
        out_specs=hbm,
        scratch_shapes=[
            pltpu.SMEM((3, ROWS), jnp.int32),
            pltpu.VMEM((2 * RINGZ, ROWS, QW), BF),
            pltpu.VMEM((KPOS, HEAD), BF),
            pltpu.VMEM((SHARD, HEAD), BF),
            pltpu.VMEM((BLK, VPOS), BF),
            pltpu.VMEM((128, HEAD), BF),
            pltpu.VMEM((2, 2, ROWS, QH), BF),
            pltpu.VMEM((4, HEADS * HEAD, COLS), BF),
            pltpu.VMEM((KPOS, 2 * QH), F32),
            pltpu.VMEM((KPOS, 2 * QH), F32),
            pltpu.VMEM((VPOS, 2 * QH), BF),
            pltpu.VMEM((8, 2 * QH), F32),
            pltpu.VMEM((8, 2 * QH), F32),
            pltpu.VMEM((2 * RINGZ, BLK, QH), BF),
            pltpu.VMEM((RINGZ, BLK, QH), BF),
            pltpu.VMEM((RINGZ, BLK, QH), BF),
            pltpu.VMEM((RINGZ, BLK, QH), BF),
            pltpu.VMEM((RINGZ, BLK, QH), BF),
            pltpu.VMEM((ROWS, HEADS * HEAD), BF),
            pltpu.VMEM((RINGZ, ROWS, HEADS * HEAD), BF),
            pltpu.VMEM((4, RINGZ, ROWS, COLS), BF),
            dma((9,)), dma((6,)), dma((6,)), dma((9,)), dma((9,)),
            dma((RINGZ,)), dma((2 * RINGZ,)), dma((RINGZ,)),
            dma((RINGZ,)), dma((RINGZ,)), dma((RINGZ,)), dma((RINGZ,)), dma((RINGZ,)),
            dma((RINGZ,)), dma((RINGZ,)), dma((4 * RINGZ,)), dma((4 * RINGZ,)),
        ],
        compiler_params=pltpu.CompilerParams(
            collective_id=0, has_side_effects=True, vmem_limit_bytes=62 * 2**20
        ),
        cost_estimate=pl.CostEstimate(
            flops=9 * 10**9, bytes_accessed=2 * 2**20, transcendentals=2048 * 4224
        ),
    )(q, k, v, ck, cv, length, branch, depth, w)
    terms = terms.reshape(RINGZ, 4 * ROWS, COLS).astype(F32)
    return jnp.sum(terms, axis=0).astype(BF)


def solution(mesh):
    in_specs = (
        P("ctx", "kvh"),
        P("ctx", "kvh"),
        P("ctx", "kvh"),
        P("ctx", "kvh"),
        P("ctx", "kvh"),
        P("ctx"),
        P("ctx"),
        P("ctx"),
        P("kvh", "ctx"),
    )
    return jax.shard_map(
        local, mesh=mesh, in_specs=in_specs, out_specs=P("kvh", "ctx"), check_vma=False
    )
```
